32 devices in a mesh: parts: 2 (over y), img: 4 (over z), wa: 2 (over x), blk: 2 (over core).
Axes of the slice: x: 2, y: 2, z: 4, core: 2. Of those that a mesh axis runs over, the one named last changes fastest.
Arguments:
- visibilities: bfloat16 [2, 8, 2, 2, 32, 128], P(None, ('parts', 'img'), 'wa', 'blk'), parts along dimension 1, may hold values from -12 to 12
- row_kernel: bfloat16 [8, 2, 2, 32, 256, 128], P(('parts', 'img'), 'wa', 'blk'), parts along dimension 0, may hold values from -6 to 6
- col_kernel: bfloat16 [8, 2, 2, 32, 128, 128], P(('parts', 'img'), 'wa', 'blk'), parts along dimension 0, may hold values from -0.5 to 0.5
- block_mask: int32 [8, 2, 2, 32, 8, 128], P(('parts', 'img'), 'wa', 'blk'), parts along dimension 0, may hold values 0 or 1
- tile_counts: int32 [8, 2, 2, 32], P(('parts', 'img'), 'wa', 'blk'), parts along dimension 0, may hold values from 1 to 128, 2048 in all within a row
- tile_ids: int32 [8, 2, 2, 32], P(('parts', 'img'), 'wa', 'blk'), parts along dimension 0, may hold values from 0 to 7
- tile_planes: int32 [8, 2, 2, 32], P(('parts', 'img'), 'wa', 'blk'), parts along dimension 0, may hold values from 0 to 1
- w_values: float32 [8], P(('parts', 'wa')), parts along dimension 0, may hold values from -40 to 40
Outputs:
- image: float32 [2048, 1024], P(('parts', 'wa', 'blk'), 'img'), parts along dimension 0
The draws below stay inside these ranges and needn't reach their ends.
There are 2 independent parts, one for each index of `parts`. The reference program is written for one: setup_inputs(seed, part) draws one part's arguments, and reference() takes and returns one part's arrays. A program takes and returns all parts, laid end to end along the dimension named above; each array names one. Nothing has to cross between parts.
All inputs are finite; a program needn't handle non-finite values. No bound on the sum of `block_mask` on one device may be relied on, other than what follows from the above.
Results may differ from the reference program's by a relative error of at most 0.013.
Values may be sent and summed in bfloat16 or wider, within the bound.
No kernel may reach another device: no remote copies, remote signals or barrier semaphores. Data moves between devices by JAX's collectives and lax.ppermute only.
A program may use at most 320 MiB of HBM per device.

```python
import math
import jax
import jax.numpy as jnp
import numpy as np
from jax import lax

SLOTS = 32
VIS = 128
PLANES = 2
TILE_W = 128
NV = 1024
ROWS = 256
NU = 1024
WPL = 4
N_IMG = 4
N_WA = 2
N_BLK = 2


def touch_ends(values, key, low, top_value):
    shape = values.shape
    index_at = [jax.random.randint(jax.random.fold_in(key, axis), (), 0, shape[axis]) for axis in range(len(shape))]
    values = values.at[tuple(index_at)].set(low)
    longest = shape.index(max(shape))
    index_at[longest] = (index_at[longest] + 1) % shape[longest]
    return values.at[tuple(index_at)].set(top_value)


def shard_levels(key, extent, cuts, smallest, top_value):
    factor_of, own = 1.0, jax.random.fold_in(key, 6)
    for dim, blocks in cuts:
        draws = jnp.exp(jax.random.uniform(jax.random.fold_in(own, dim), (blocks,), jnp.float32, smallest / len(cuts), top_value / len(cuts)))
        factor_of = factor_of * jnp.repeat(draws, extent[dim] // blocks).reshape([-1 if axis == dim else 1 for axis in range(len(extent))])
    return factor_of


def profile(count, total, bound, skew):
    loads = [(1 << 20) // math.isqrt(rank ** skew) + 1 for rank in range(2, count + 1)]
    rest, given = total - bound - (count - 1), [1] * (count - 1)
    while rest > 0:
        movable = [i for i in range(count - 1) if given[i] < bound]
        mass, remaining = sum([loads[i] for i in movable]), rest
        for i in movable:
            more = min(bound - given[i], max(1, remaining * loads[i] // mass), rest)
            given[i] = given[i] + more
            rest = rest - more
    return np.array([bound] + given)


def ragged(key, amount, total, limit, skew):
    if amount == 2:
        one = jax.random.randint(key, (), max(1, total - limit), min(limit, total - 1) + 1)
        return jnp.stack([one, total - one])
    sizes = jnp.asarray(profile(amount, total, limit, skew), jnp.int32)
    couples = (amount - 1) // 2
    source_of, taker = sizes[1:1 + 2 * couples:2], sizes[2:2 + 2 * couples:2]
    slack = jnp.minimum(source_of - 1, limit - taker)
    shifted = jax.random.randint(jax.random.fold_in(key, 1), (couples,), 0, 1 << 20) % (slack + 1)
    sizes = sizes.at[1:1 + 2 * couples:2].set(source_of - shifted).at[2:2 + 2 * couples:2].set(taker + shifted)
    return sizes[jax.random.permutation(jax.random.fold_in(key, 2), amount)]


def bell_draw(stream_key, extent, scale, limit, split=(), kind=jnp.bfloat16):
    entries = jax.random.normal(stream_key, extent, jnp.float32) * scale
    if len(split) > 0:
        entries = shard_levels(stream_key, extent, split, -0.22, 0.18) * entries
    return jnp.clip(entries, min=-limit, max=limit).astype(kind)


def setup_inputs(seed: int = 0, part: int = 0) -> dict:
    keys = jax.random.split(jax.random.key(seed), 9)
    part_splits = jax.random.split(jax.random.fold_in(keys[8], part), 9)
    visibilities = bell_draw(part_splits[0], (2, N_IMG, N_WA, N_BLK, SLOTS, VIS), 2.0, 12.0, ((1, 4), (2, 2), (3, 2)))
    row_kernel = bell_draw(part_splits[1], (N_IMG, N_WA, N_BLK, SLOTS, ROWS, VIS), 1.0, 6.0, ((0, 4), (1, 2), (2, 2)))
    col_kernel = bell_draw(part_splits[2], (N_IMG, N_WA, N_BLK, SLOTS, VIS, TILE_W), VIS ** -0.5, 0.5, ((0, 4), (1, 2), (2, 2)))
    block_mask = touch_ends((jax.random.randint(part_splits[3], (N_IMG, N_WA, N_BLK, SLOTS, TILE_W // 16, VIS), 0, 2) < 1).astype(jnp.int32), jax.random.fold_in(part_splits[3], 1), 0, 1)
    tile_counts = jax.vmap(lambda own: ragged(own, SLOTS, SLOTS * VIS // 2, VIS, 2))(jax.random.split(part_splits[4], N_IMG * N_WA * N_BLK)).reshape((N_IMG, N_WA, N_BLK, SLOTS)).astype(jnp.int32)
    tile_ids = touch_ends(jax.random.randint(part_splits[5], (N_IMG, N_WA, N_BLK, SLOTS), 0, NV // TILE_W), jax.random.fold_in(part_splits[5], 1), 0, (NV // TILE_W) - 1).astype(jnp.int32)
    tile_planes = touch_ends(jax.random.randint(part_splits[6], (N_IMG, N_WA, N_BLK, SLOTS), 0, PLANES), jax.random.fold_in(part_splits[6], 1), 0, PLANES - 1).astype(jnp.int32)
    w_values = jnp.clip(jax.random.uniform(part_splits[7], (WPL,), jnp.float32, -40.0, 40.0) * shard_levels(part_splits[7], (WPL,), ((0, 2),), -0.4, 0.0), -40.0, 40.0)
    return dict(visibilities=visibilities, row_kernel=row_kernel, col_kernel=col_kernel, block_mask=block_mask, tile_counts=tile_counts, tile_ids=tile_ids, tile_planes=tile_planes, w_values=w_values)


def reference(visibilities, row_kernel, col_kernel, block_mask, tile_counts, tile_ids, tile_planes, w_values):
    across = NV // TILE_W
    precise = lax.Precision.HIGHEST

    def slab(pieces):
        vis, rker, cker, masks, counts, idents, levels = pieces
        live = (jnp.arange(VIS)[None, None, None, :] < counts[..., None]).astype(jnp.float32)
        mask_cols = jnp.repeat(jnp.swapaxes(masks, -1, -2).astype(jnp.float32), 16, axis=-1)
        weighted = ((vis.astype(jnp.float32) * live)[..., None] * (cker.astype(jnp.float32) * mask_cols)[None]).astype(jnp.bfloat16)
        tiles = jnp.einsum('wbsap,cwbspk->wbscak', rker.astype(jnp.float32), weighted.astype(jnp.float32), precision=precise)
        codes = levels * across + idents
        onehot = (codes[..., None] == jnp.arange(PLANES * across)[None, None, None, :]).astype(jnp.float32)
        onehot = onehot.reshape(N_WA, N_BLK, SLOTS, PLANES, across)
        partial_value = jnp.einsum('wbspt,wbscak->wbcpatk', onehot, tiles, precision=precise)
        partial_value = lax.optimization_barrier(partial_value.astype(jnp.bfloat16)).astype(jnp.float32)
        summed = lax.optimization_barrier(jnp.sum(partial_value, axis=1))
        summed = jnp.transpose(summed, (1, 0, 2, 3, 4, 5))
        return summed.reshape(2, N_WA * PLANES, ROWS, NV)
    slabs = lax.map(slab, (jnp.moveaxis(visibilities, 1, 0), row_kernel, col_kernel, block_mask, tile_counts, tile_ids, tile_planes))
    grid = jnp.transpose(slabs, (1, 2, 0, 3, 4)).reshape(2, N_WA * PLANES, NU, NV)
    xcoord = (jnp.arange(NU).astype(jnp.float32) - NU / 2) / NU
    ycoord = (jnp.arange(NV).astype(jnp.float32) - NV / 2) / NV
    nterm = jnp.sqrt(1.0 - xcoord[:, None] ** 2 - ycoord[None, :] ** 2) - 1.0

    def plane_step(total, item):
        real, imag, wval = item
        field = jnp.fft.ifft2(real + 1j * imag) * (NU * NV)
        phase = 2.0 * math.pi * wval * nterm
        return (total + jnp.cos(phase) * field.real - jnp.sin(phase) * field.imag, None)
    start = jnp.zeros((NU, NV), jnp.float32)
    total, unused = lax.scan(plane_step, start, (grid[0], grid[1], w_values))
    return total / math.sqrt(NU * NV * N_WA * PLANES)
```

```python
import functools
import math

import jax
import jax.numpy as jnp
import numpy as np
from jax import lax
from jax.experimental import pallas as pl
from jax.experimental.pallas import tpu as pltpu
from jax.sharding import PartitionSpec as P

NV = 1024
LANES = 128
VMEM = pltpu.VMEM
SMEM = pltpu.SMEM


def angles(first, second, length):
    return 2.0 * np.pi / length * (np.outer(first, second) % length)


def row_table(across, tile_width):
    half_v = np.arange(NV // 2)
    out = []
    for parity in range(2):
        m_index = 2 * np.arange(NV // 2) + parity
        ang = angles(half_v, m_index, NV)
        cosine, sine = np.cos(ang), np.sin(ang)
        real = np.stack([cosine, -sine])
        imag = np.stack([sine, cosine])
        both = np.stack([real, imag])
        both = both.reshape(2, 2, across // 2, tile_width, NV // 2 // LANES, LANES)
        out.append(both.transpose(2, 1, 3, 4, 0, 5).reshape(NV, NV))
    return np.stack(out)


def column_table(img_count, rows):
    full = img_count * rows
    ang = angles(np.arange(full // 2), np.arange(full), full)
    cosine, sine = np.cos(ang), np.sin(ang)
    sine[0] = np.cos(np.pi * (np.arange(full) % 2))
    both = np.stack([cosine, sine]).reshape(2, full // 2, img_count, rows)
    return both.transpose(2, 0, 1, 3)


def grid_kernel(
    group, counts_ref, ids_ref, planes_ref, vis_ref, mask_ref, rk_ref, ck_ref, own_ref, send_ref, acc
):
    step = pl.program_id(0)
    codes, rows, _ = acc.shape
    width = ck_ref.shape[2]
    vis_len = ck_ref.shape[1]
    blocks = mask_ref.shape[1]
    planes = own_ref.shape[0]
    across = codes // planes

    @pl.when(step == 0)
    def _():
        acc[...] = jnp.zeros_like(acc)

    lane = lax.broadcasted_iota(jnp.int32, (1, vis_len), 1)
    row_of = lax.broadcasted_iota(jnp.int32, (2 * blocks, 2 * width), 0)
    col_of = lax.broadcasted_iota(jnp.int32, (2 * blocks, 2 * width), 1)
    spread = (row_of == col_of // (width // blocks)).astype(jnp.bfloat16)
    for pair in range(group // 2):
        stacked = []
        for one in range(2):
            s = 2 * pair + one
            slot = step * group + s
            live = (lane < counts_ref[slot]).astype(jnp.float32)
            mask = mask_ref[s].astype(jnp.float32) * live
            real = mask * vis_ref[0, pl.ds(s, 1), :].astype(jnp.float32)
            imag = mask * vis_ref[1, pl.ds(s, 1), :].astype(jnp.float32)
            stacked.append(jnp.concatenate([real, imag], axis=1))
        left = jnp.concatenate(stacked, axis=0).astype(jnp.bfloat16)
        scale = lax.dot_general(
            left, spread, (((0,), (0,)), ((), ())), preferred_element_type=jnp.float32
        ).astype(jnp.bfloat16)
        for one in range(2):
            s = 2 * pair + one
            slot = step * group + s
            cols = ck_ref[s]
            part = scale[:, one * width : (one + 1) * width]
            weighted = jnp.concatenate([part[:vis_len] * cols, part[vis_len:] * cols], axis=1)
            tile = jnp.dot(rk_ref[s], weighted, preferred_element_type=jnp.float32)
            code = planes_ref[slot] * across + ids_ref[slot]
            acc[code] += tile

    @pl.when(step == pl.num_programs(0) - 1)
    def _():
        sign = (1 - 2 * lax.axis_index("blk")).astype(jnp.float32)
        for plane in range(planes):
            for t in range(across // 2):
                low = acc[plane * across + t]
                high = acc[plane * across + t + across // 2] * sign
                where = pl.ds(t * 2 * width, 2 * width)
                own_ref[plane, :, where] = low + high
                send_ref[plane, :, where] = (low - high).astype(jnp.bfloat16)


def gridding(counts, ids, levels, vis, mask, rk, ck, planes):
    slots, rows, vis_len = rk.shape
    width = ck.shape[2]
    across = NV // width
    group = 8
    half = (planes, rows, NV)
    return pl.pallas_call(
        functools.partial(grid_kernel, group),
        grid=(slots // group,),
        in_specs=[pl.BlockSpec(memory_space=SMEM)] * 3
        + [
            pl.BlockSpec((2, group, vis_len), lambda g: (0, g, 0)),
            pl.BlockSpec((group,) + mask.shape[1:], lambda g: (g, 0, 0)),
            pl.BlockSpec((group, rows, vis_len), lambda g: (g, 0, 0)),
            pl.BlockSpec((group, vis_len, width), lambda g: (g, 0, 0)),
        ],
        out_specs=[pl.BlockSpec(half, lambda g: (0, 0, 0))] * 2,
        out_shape=[
            jax.ShapeDtypeStruct(half, jnp.float32),
            jax.ShapeDtypeStruct(half, jnp.bfloat16),
        ],
        scratch_shapes=[VMEM((planes * across, rows, 2 * width), jnp.float32)],
        compiler_params=pltpu.CompilerParams(vmem_limit_bytes=24 << 20),
        name="gridding",
    )(counts, ids, levels, vis, mask, rk, ck)


def row_kernel_body(own_ref, recv_ref, table_ref, out_ref, table, sem):
    copy = pltpu.make_async_copy(table_ref.at[lax.axis_index("blk")], table, sem)
    copy.start()
    planes, rows, _ = own_ref.shape
    grid = (own_ref[...] + recv_ref[...].astype(jnp.float32)).astype(jnp.bfloat16)
    grid = grid.reshape(planes * rows, NV)
    copy.wait()
    for g in range(out_ref.shape[0]):
        part = jnp.dot(
            grid, table[:, g * 2 * LANES : (g + 1) * 2 * LANES], preferred_element_type=jnp.float32
        )
        out_ref[g] = part.astype(jnp.bfloat16).reshape(planes, rows, 2 * LANES)


def row_transform(own, recv, table):
    planes, rows, _ = own.shape
    groups = NV // 2 // LANES
    return pl.pallas_call(
        row_kernel_body,
        in_specs=[
            pl.BlockSpec(memory_space=VMEM),
            pl.BlockSpec(memory_space=VMEM),
            pl.BlockSpec(memory_space=pl.ANY),
        ],
        out_specs=pl.BlockSpec(memory_space=VMEM),
        out_shape=jax.ShapeDtypeStruct((groups, planes, rows, 2 * LANES), jnp.bfloat16),
        scratch_shapes=[VMEM((NV, NV), jnp.bfloat16), pltpu.SemaphoreType.DMA],
        compiler_params=pltpu.CompilerParams(vmem_limit_bytes=24 << 20),
        name="row_dft",
    )(own, recv, table)


COS_POLY = np.polynomial.chebyshev.Chebyshev.interpolate(
    lambda z: np.cos(2 * np.pi * np.sqrt(np.maximum(z, 0.0))), 6, [0.0, 0.25]
).convert(kind=np.polynomial.Polynomial).coef
SIN_POLY = np.polynomial.chebyshev.Chebyshev.interpolate(
    lambda z: np.sinc(2 * np.sqrt(np.maximum(z, 0.0))) * 2 * np.pi, 6, [0.0, 0.25]
).convert(kind=np.polynomial.Polynomial).coef


def horner(coef, z):
    total = jnp.full_like(z, float(coef[-1]))
    for value in coef[-2::-1]:
        total = total * z + float(value)
    return total


def turn(cycles):
    rest = cycles - jnp.round(cycles)
    square = rest * rest
    return horner(COS_POLY, square), horner(SIN_POLY, square) * rest


def column_kernel(rotate, w_ref, rows_ref, table_ref, out_ref, table, back, sem):
    img = lax.axis_index("img")
    wa = lax.axis_index("wa")
    blk = lax.axis_index("blk")
    copy = pltpu.make_async_copy(table_ref.at[img], table, sem)
    copy.start()
    groups, planes = rows_ref.shape[0], rows_ref.shape[1]
    wa_count, piece = out_ref.shape[0], out_ref.shape[2]
    half = table.shape[1]
    full = 2 * half
    block = LANES
    row_at = lax.broadcasted_iota(jnp.int32, (half, half), 0)
    col_at = lax.broadcasted_iota(jnp.int32, (half, half), 1)
    flip = (row_at == jnp.where(col_at == 0, 0, half - col_at)).astype(jnp.bfloat16)
    copy.wait()

    def put(start, count, g, value):
        for j in range(count // piece):
            at = lax.rem(start // piece + j - wa + wa_count, wa_count)
            out_ref[at, g] = value[j * piece : (j + 1) * piece]

    for k in range(groups):
        g = lax.rem(img + k, groups) if rotate else k
        column = 2 * (g * LANES + lax.broadcasted_iota(jnp.int32, (1, LANES), 1)) + blk
        y = (column.astype(jnp.float32) - NV / 2) / NV
        rest_y = 1.0 - y * y
        firsts = []
        for start in range(0, half, block):
            row = start + lax.broadcasted_iota(jnp.int32, (block, 1), 0)
            x = (row.astype(jnp.float32) - half) / full
            nterm = jnp.sqrt(rest_y - x * x) - 1.0
            even = jnp.zeros((block, LANES), jnp.float32)
            odd = jnp.zeros((block, LANES), jnp.float32)
            for q in range(planes):
                rhs = rows_ref[g, q]
                by_cos = jnp.dot(
                    table[0, start : start + block], rhs, preferred_element_type=jnp.float32
                )
                by_sin = jnp.dot(
                    table[1, start : start + block], rhs, preferred_element_type=jnp.float32
                )
                cosine, sine = turn(nterm * w_ref[q])
                even += cosine * by_cos[:, :LANES] - sine * by_cos[:, LANES:]
                if start == 0:
                    mid_c, mid_s = turn((jnp.sqrt(rest_y) - 1.0) * w_ref[q])
                    cosine, sine = (
                        jnp.where(row == 0, -mid_s, cosine),
                        jnp.where(row == 0, mid_c, sine),
                    )
                odd += cosine * by_sin[:, LANES:] + sine * by_sin[:, :LANES]
            low, high = even - odd, even + odd
            if start == 0:
                low = jnp.where(row == 0, even, low)
                high = jnp.where(row == 0, odd, high)
            firsts.append(low.astype(jnp.bfloat16))
            back[start : start + block] = high.astype(jnp.bfloat16)
        put(0, half, k, jnp.concatenate(firsts, axis=0))
        second = jnp.dot(flip, back[...], preferred_element_type=jnp.float32).astype(jnp.bfloat16)
        put(half, half, k, second)


def column_transform(w_values, rowdft, table, wa_count, rotate):
    groups, planes, rows, _ = rowdft.shape
    half = table.shape[2]
    return pl.pallas_call(
        functools.partial(column_kernel, rotate),
        in_specs=[
            pl.BlockSpec(memory_space=SMEM),
            pl.BlockSpec(memory_space=VMEM),
            pl.BlockSpec(memory_space=pl.ANY),
        ],
        out_specs=pl.BlockSpec(memory_space=VMEM),
        out_shape=jax.ShapeDtypeStruct(
            (wa_count, groups, 2 * half // wa_count, LANES), jnp.bfloat16
        ),
        scratch_shapes=[
            VMEM(table.shape[1:], jnp.bfloat16),
            VMEM((half, LANES), jnp.bfloat16),
            pltpu.SemaphoreType.DMA,
        ],
        compiler_params=pltpu.CompilerParams(vmem_limit_bytes=24 << 20),
        name="column_dft",
    )(w_values, rowdft, table)


def add_up(*parts):
    return sum(part.astype(jnp.float32) for part in parts)


def shift(value, axis, by):
    count = lax.axis_size(axis)
    return lax.ppermute(value, axis, [(one, (one + by) % count) for one in range(count)])


def shards(
    visibilities, row_kernel, col_kernel, block_mask, tile_counts, tile_ids, tile_planes, w_values
):
    slots = tile_counts.shape[3]
    planes = w_values.shape[0]
    rows, vis_len = row_kernel.shape[4], row_kernel.shape[5]
    width = col_kernel.shape[5]
    img_count = lax.axis_size("img")
    wa_count = lax.axis_size("wa")
    full = rows * img_count
    table_r = jnp.asarray(row_table(NV // width, width), jnp.bfloat16)
    table_c = jnp.asarray(column_table(img_count, rows), jnp.bfloat16)
    own, send = gridding(
        tile_counts.reshape(slots),
        tile_ids.reshape(slots),
        tile_planes.reshape(slots),
        visibilities.reshape(2, slots, vis_len),
        block_mask.reshape(slots, -1, vis_len),
        row_kernel.reshape(slots, rows, vis_len),
        col_kernel.reshape(slots, vis_len, width),
        planes,
    )
    rowdft = row_transform(own, shift(send, "blk", 1), table_r)
    groups = rowdft.shape[0]
    rotate = groups == img_count
    image = column_transform(w_values, rowdft, table_c, wa_count, rotate)
    held = add_up(image[0], *(shift(image[by], "wa", by) for by in range(1, wa_count)))
    held = held.astype(jnp.bfloat16)
    if not rotate:
        held = jnp.swapaxes(held, 0, 1).reshape(full // wa_count, img_count, -1)
        held = jnp.roll(jnp.swapaxes(held, 0, 1), -lax.axis_index("img"), axis=0)
    total = add_up(held[0], *(shift(held[by], "img", by) for by in range(1, img_count)))
    blk = lax.axis_index("blk")
    total = total.reshape(2, total.shape[0] // 2, total.shape[1])
    mine = lax.dynamic_index_in_dim(total, blk, 0, keepdims=False)
    other = lax.dynamic_index_in_dim(total, 1 - blk, 0, keepdims=False)
    other = shift(other.astype(jnp.bfloat16), "blk", 1).astype(jnp.float32)
    count = mine.shape[1]
    source = jnp.arange(2 * count, dtype=jnp.int32)
    target = jnp.where(source < count, 2 * source + blk, 2 * (source - count) + 1 - blk)
    place = (target[:, None] == jnp.arange(2 * count, dtype=jnp.int32)[None, :]).astype(jnp.float32)
    both = jnp.concatenate([mine, other], axis=1)
    scale = 1.0 / math.sqrt(full * NV * planes * wa_count)
    return jnp.dot(both, place, precision=lax.Precision.HIGHEST) * scale


def solution(mesh):
    in_specs = (
        P(None, ("parts", "img"), "wa", "blk", None, None),
        P(("parts", "img"), "wa", "blk", None, None, None),
        P(("parts", "img"), "wa", "blk", None, None, None),
        P(("parts", "img"), "wa", "blk", None, None, None),
        P(("parts", "img"), "wa", "blk", None),
        P(("parts", "img"), "wa", "blk", None),
        P(("parts", "img"), "wa", "blk", None),
        P(("parts", "wa")),
    )
    out_specs = P(("parts", "wa", "blk"), "img")
    return jax.shard_map(shards, mesh=mesh, in_specs=in_specs, out_specs=out_specs, check_vma=False)
```

```python
import functools
import math

import jax
import jax.numpy as jnp
import numpy as np
from jax import lax
from jax.experimental import pallas as pl
from jax.experimental.pallas import tpu as pltpu
from jax.sharding import PartitionSpec as P

NV = 1024
LANES = 128
VMEM = pltpu.VMEM
SMEM = pltpu.SMEM
HBM = pltpu.HBM


def angles(first, second, length):
    return 2.0 * np.pi / length * (np.outer(first, second) % length)


def row_table(across, tile_width):
    half_v = np.arange(NV // 2)
    out = []
    for parity in range(2):
        m_index = 2 * np.arange(NV // 2) + parity
        ang = angles(half_v, m_index, NV)
        cosine, sine = np.cos(ang), np.sin(ang)
        real = np.stack([cosine, -sine])
        imag = np.stack([sine, cosine])
        both = np.stack([real, imag])
        both = both.reshape(2, 2, across // 2, tile_width, NV // 2 // LANES, LANES)
        out.append(both.transpose(4, 2, 1, 3, 0, 5).reshape(-1, NV, 2 * LANES))
    return np.stack(out)


def column_table(img_count, rows):
    full = img_count * rows
    ang = angles(np.arange(full // 2), np.arange(full), full)
    cosine, sine = np.cos(ang), np.sin(ang)
    sine[0] = np.cos(np.pi * (np.arange(full) % 2))
    both = np.stack([cosine, sine]).reshape(2, full // 2, img_count, rows)
    return both.transpose(2, 0, 1, 3)


def grid_kernel(
    counts_hbm,
    ids_hbm,
    planes_hbm,
    vis_hbm,
    mask_hbm,
    rk_hbm,
    ck_hbm,
    own_ref,
    send_ref,
    counts_ref,
    ids_ref,
    planes_ref,
    vis_ref,
    mask_ref,
    rk_ref,
    ck_ref,
    acc,
    small_sem,
    rk_sem,
    ck_sem,
):
    blk = lax.axis_index("blk")
    slots, rows, vis_len = rk_ref.shape
    codes = acc.shape[0]
    width = ck_ref.shape[2]
    blocks = mask_ref.shape[1]
    planes = own_ref.shape[0]
    across = codes // planes
    chunks = rk_sem.shape[0]
    group = slots // chunks

    small = [
        pltpu.make_async_copy(source, target, small_sem.at[n])
        for n, (source, target) in enumerate(
            [
                (counts_hbm, counts_ref),
                (ids_hbm, ids_ref),
                (planes_hbm, planes_ref),
                (vis_hbm, vis_ref),
                (mask_hbm, mask_ref),
            ]
        )
    ]
    large = []
    for n in range(chunks):
        part = pl.ds(n * group, group)
        large.append(
            [
                pltpu.make_async_copy(ck_hbm.at[part], ck_ref.at[part], ck_sem.at[n]),
                pltpu.make_async_copy(rk_hbm.at[part], rk_ref.at[part], rk_sem.at[n]),
            ]
        )
    for copy in small + sum(large, []):
        copy.start()
    acc[...] = jnp.zeros_like(acc)
    for copy in small:
        copy.wait()

    lane = lax.broadcasted_iota(jnp.int32, (1, vis_len), 1)
    real, imag = [], []
    for slot in range(slots):
        mask = mask_ref[slot].astype(jnp.float32) * (lane < counts_ref[slot]).astype(jnp.float32)
        real.append(mask * vis_ref[0, pl.ds(slot, 1), :].astype(jnp.float32))
        imag.append(mask * vis_ref[1, pl.ds(slot, 1), :].astype(jnp.float32))
    scaled = jnp.concatenate(
        [jnp.concatenate(real, axis=0).T, jnp.concatenate(imag, axis=0).T], axis=0
    ).astype(jnp.bfloat16)
    row_of = lax.broadcasted_iota(jnp.int32, (slots * blocks, 2 * width), 0)
    block_of = lax.broadcasted_iota(jnp.int32, (slots * blocks, 2 * width), 1) // (width // blocks)
    behind = row_of - block_of
    for pair in range(slots // 2):
        if 2 * pair % group == 0:
            for copy in large[2 * pair // group]:
                copy.wait()
        spread = (behind == 2 * pair * blocks).astype(jnp.bfloat16)
        scale = jnp.dot(scaled, spread, preferred_element_type=jnp.float32).astype(jnp.bfloat16)
        for slot in (2 * pair, 2 * pair + 1):
            cols = ck_ref[slot]
            part = scale[:, (slot % 2) * width : (slot % 2 + 1) * width]
            weighted = jnp.concatenate([part[:vis_len] * cols, part[vis_len:] * cols], axis=1)
            tile = jnp.dot(rk_ref[slot], weighted, preferred_element_type=jnp.float32)
            code = planes_ref[slot] * across + ids_ref[slot]
            acc[code] += tile

    sign = (1 - 2 * blk).astype(jnp.float32)
    for plane in range(planes):
        for t in range(across // 2):
            low = acc[plane * across + t]
            high = acc[plane * across + t + across // 2] * sign
            where = pl.ds(t * 2 * width, 2 * width)
            own_ref[plane, :, where] = low + high
            send_ref[plane, :, where] = (low - high).astype(jnp.bfloat16)


def gridding(counts, ids, levels, vis, mask, rk, ck, planes):
    slots, rows, vis_len = rk.shape
    width = ck.shape[2]
    across = NV // width
    chunks = 4
    half = (planes, rows, NV)
    inputs = (counts, ids, levels, vis, mask, rk, ck)
    return pl.pallas_call(
        grid_kernel,
        in_specs=[pl.BlockSpec(memory_space=HBM)] * len(inputs),
        out_specs=[pl.BlockSpec(memory_space=VMEM)] * 2,
        out_shape=[
            jax.ShapeDtypeStruct(half, jnp.float32),
            jax.ShapeDtypeStruct(half, jnp.bfloat16),
        ],
        scratch_shapes=[SMEM(counts.shape, jnp.int32)] * 3
        + [VMEM(value.shape, value.dtype) for value in (vis, mask, rk, ck)]
        + [
            VMEM((planes * across, rows, 2 * width), jnp.float32),
            pltpu.SemaphoreType.DMA((5,)),
            pltpu.SemaphoreType.DMA((chunks,)),
            pltpu.SemaphoreType.DMA((chunks,)),
        ],
        compiler_params=pltpu.CompilerParams(vmem_limit_bytes=24 << 20),
        name="gridding",
    )(*(pltpu.with_memory_space_constraint(value, HBM) for value in inputs))


COS_POLY = np.polynomial.chebyshev.Chebyshev.interpolate(
    lambda z: np.cos(2 * np.pi * np.sqrt(np.maximum(z, 0.0))), 6, [0.0, 0.25]
).convert(kind=np.polynomial.Polynomial).coef
SIN_POLY = np.polynomial.chebyshev.Chebyshev.interpolate(
    lambda z: np.sinc(2 * np.sqrt(np.maximum(z, 0.0))) * 2 * np.pi, 6, [0.0, 0.25]
).convert(kind=np.polynomial.Polynomial).coef


def horner(coef, z):
    total = jnp.full_like(z, float(coef[-1]))
    for value in coef[-2::-1]:
        total = total * z + float(value)
    return total


def turn(cycles):
    rest = cycles - jnp.round(cycles)
    square = rest * rest
    return horner(COS_POLY, square), horner(SIN_POLY, square) * rest


def screen_kernel(
    w_ref, table_r_hbm, table_c_hbm, screen_ref, middle_ref, table_r_ref, table_c_ref, sem
):
    copies = [
        pltpu.make_async_copy(table_r_hbm.at[lax.axis_index("blk")], table_r_ref, sem.at[0]),
        pltpu.make_async_copy(table_c_hbm.at[lax.axis_index("img")], table_c_ref, sem.at[1]),
    ]
    for copy in copies:
        copy.start()
    planes, groups, half, _ = screen_ref.shape
    full = 2 * half
    blk = lax.axis_index("blk")
    block = LANES
    for g in range(groups):
        column = 2 * (g * LANES + lax.broadcasted_iota(jnp.int32, (1, LANES), 1)) + blk
        y = (column.astype(jnp.float32) - NV / 2) / NV
        rest_y = 1.0 - y * y
        for q in range(planes):
            cosine, sine = turn((jnp.sqrt(rest_y) - 1.0) * w_ref[q])
            middle_ref[q, g] = jnp.concatenate([cosine, sine], axis=1)
        for start in range(0, half, block):
            row = start + lax.broadcasted_iota(jnp.int32, (block, 1), 0)
            x = (row.astype(jnp.float32) - half) / full
            nterm = jnp.sqrt(rest_y - x * x) - 1.0
            for q in range(planes):
                cosine, sine = turn(nterm * w_ref[q])
                screen_ref[q, g, start : start + block, :LANES] = cosine
                screen_ref[q, g, start : start + block, LANES:] = sine
    for copy in copies:
        copy.wait()


def screens(w_values, table_r, table_c):
    planes = w_values.shape[0]
    groups = table_r.shape[1]
    half = table_c.shape[2]
    tables = [pltpu.with_memory_space_constraint(value, HBM) for value in (table_r, table_c)]
    return pl.pallas_call(
        screen_kernel,
        in_specs=[pl.BlockSpec(memory_space=SMEM)] + [pl.BlockSpec(memory_space=HBM)] * 2,
        out_specs=[pl.BlockSpec(memory_space=VMEM)] * 4,
        out_shape=[
            jax.ShapeDtypeStruct((planes, groups, half, 2 * LANES), jnp.float32),
            jax.ShapeDtypeStruct((planes, groups, 1, 2 * LANES), jnp.float32),
            jax.ShapeDtypeStruct(table_r.shape[1:], jnp.bfloat16),
            jax.ShapeDtypeStruct(table_c.shape[1:], jnp.bfloat16),
        ],
        scratch_shapes=[pltpu.SemaphoreType.DMA((2,))],
        compiler_params=pltpu.CompilerParams(vmem_limit_bytes=24 << 20),
        cost_estimate=pl.CostEstimate(
            flops=planes * half * NV * 20, bytes_accessed=planes * half * NV * 4, transcendentals=0
        ),
        name="screens",
    )(w_values, *tables)


def image_kernel(offsets, rotate, own_ref, recv_ref, table_r, table_c, screen_ref, middle_ref, *refs):
    outs, (rowdft, back) = refs[:-2], refs[-2:]
    planes, rows, _ = own_ref.shape
    groups = screen_ref.shape[1]
    grid = (own_ref[...] + recv_ref[...].astype(jnp.float32)).astype(jnp.bfloat16)
    grid = grid.reshape(planes * rows, NV)
    for g in range(groups):
        rowdft[g] = jnp.dot(grid, table_r[g], preferred_element_type=jnp.float32).astype(
            jnp.bfloat16
        )
    img = lax.axis_index("img")
    wa = lax.axis_index("wa")
    wa_count, piece = outs[0].shape[0], outs[0].shape[1]
    half = table_c.shape[1]
    block = LANES
    row_at = lax.broadcasted_iota(jnp.int32, (half, half), 0)
    col_at = lax.broadcasted_iota(jnp.int32, (half, half), 1)
    flip = (row_at == jnp.where(col_at == 0, 0, half - col_at)).astype(jnp.bfloat16)

    def put(start, count, n, value):
        for j in range(count // piece):
            at = lax.rem(start // piece + j - wa + wa_count, wa_count)
            outs[n][at] = value[j * piece : (j + 1) * piece]

    for n, k in enumerate(offsets):
        g = lax.rem(img + k, groups) if rotate else k
        firsts = []
        for start in range(0, half, block):
            even = jnp.zeros((block, LANES), jnp.float32)
            odd = jnp.zeros((block, LANES), jnp.float32)
            for q in range(planes):
                rhs = rowdft[g, q * rows : (q + 1) * rows]
                by_cos = jnp.dot(
                    table_c[0, start : start + block], rhs, preferred_element_type=jnp.float32
                )
                by_sin = jnp.dot(
                    table_c[1, start : start + block], rhs, preferred_element_type=jnp.float32
                )
                cosine = screen_ref[q, g, start : start + block, :LANES]
                sine = screen_ref[q, g, start : start + block, LANES:]
                even += cosine * by_cos[:, :LANES] - sine * by_cos[:, LANES:]
                if start == 0:
                    row = lax.broadcasted_iota(jnp.int32, (block, 1), 0)
                    cosine, sine = (
                        jnp.where(row == 0, -middle_ref[q, g, :, LANES:], cosine),
                        jnp.where(row == 0, middle_ref[q, g, :, :LANES], sine),
                    )
                odd += cosine * by_sin[:, LANES:] + sine * by_sin[:, :LANES]
            low, high = even - odd, even + odd
            if start == 0:
                low = jnp.where(row == 0, even, low)
                high = jnp.where(row == 0, odd, high)
            firsts.append(low.astype(jnp.bfloat16))
            back[start : start + block] = high.astype(jnp.bfloat16)
        put(0, half, n, jnp.concatenate(firsts, axis=0))
        second = jnp.dot(flip, back[...], preferred_element_type=jnp.float32).astype(jnp.bfloat16)
        put(half, half, n, second)


def images(offsets, rotate, wa_count, own, recv, screen, middle, table_r, table_c):
    half = table_c.shape[1]
    planes, rows, _ = own.shape
    inputs = (own, recv, table_r, table_c, screen, middle)
    one = jax.ShapeDtypeStruct((wa_count, 2 * half // wa_count, LANES), jnp.bfloat16)
    return pl.pallas_call(
        functools.partial(image_kernel, offsets, rotate),
        in_specs=[pl.BlockSpec(memory_space=VMEM)] * len(inputs),
        out_specs=[pl.BlockSpec(memory_space=VMEM)] * len(offsets),
        out_shape=[one] * len(offsets),
        scratch_shapes=[
            VMEM((table_r.shape[0], planes * rows, 2 * LANES), jnp.bfloat16),
            VMEM((half, LANES), jnp.bfloat16),
        ],
        compiler_params=pltpu.CompilerParams(vmem_limit_bytes=24 << 20),
        name="image",
    )(*inputs)


def add_kernel(one_ref, *refs):
    total = one_ref[...].astype(jnp.float32)
    for ref in refs[:-1]:
        total += ref[...].astype(jnp.float32)
    refs[-1][...] = total.astype(refs[-1].dtype)


def add_rounded(*parts):
    return pl.pallas_call(
        add_kernel,
        in_specs=[pl.BlockSpec(memory_space=VMEM)] * len(parts),
        out_specs=pl.BlockSpec(memory_space=VMEM),
        out_shape=jax.ShapeDtypeStruct(parts[0].shape, jnp.bfloat16),
        compiler_params=pltpu.CompilerParams(vmem_limit_bytes=24 << 20),
        name="add",
    )(*parts)


def add_up(*parts):
    return sum(part.astype(jnp.float32) for part in parts)


def shift(value, axis, by):
    count = lax.axis_size(axis)
    return lax.ppermute(value, axis, [(one, (one + by) % count) for one in range(count)])


def shards(
    visibilities, row_kernel, col_kernel, block_mask, tile_counts, tile_ids, tile_planes, w_values
):
    slots = tile_counts.shape[3]
    planes = w_values.shape[0]
    rows, vis_len = row_kernel.shape[4], row_kernel.shape[5]
    width = col_kernel.shape[5]
    img_count = lax.axis_size("img")
    wa_count = lax.axis_size("wa")
    full = rows * img_count
    table_r = jnp.asarray(row_table(NV // width, width), jnp.bfloat16)
    table_c = jnp.asarray(column_table(img_count, rows), jnp.bfloat16)
    own, send = gridding(
        tile_counts.reshape(slots),
        tile_ids.reshape(slots),
        tile_planes.reshape(slots),
        visibilities.reshape(2, slots, vis_len),
        block_mask.reshape(slots, -1, vis_len),
        row_kernel.reshape(slots, rows, vis_len),
        col_kernel.reshape(slots, vis_len, width),
        planes,
    )
    recv = shift(send, "blk", 1)
    screen, middle, table_r, table_c = screens(w_values, table_r, table_c)
    groups = screen.shape[1]
    rotate = groups == img_count
    offsets = [2, 3, 1, 0] if rotate else list(range(groups))
    parts = images(
        offsets, rotate, wa_count, own, recv, screen, middle, table_r, table_c
    )

    def over_wa(part):
        return [shift(part[by], "wa", by) for by in range(1, wa_count)]

    if rotate:
        far, before, after, here = parts
        from_after = shift(before, "img", 3)
        far = add_rounded(far[0], *over_wa(far))
        after = add_rounded(after[0], *over_wa(after))
        from_far = shift(far, "img", 2)
        from_before = shift(after, "img", 1)
        here = add_rounded(here, from_after)
        total = add_up(here[0], *over_wa(here), from_far, from_before)
    else:
        part = jnp.stack(parts, axis=1)
        held = add_rounded(part[0], *over_wa(part))
        held = jnp.swapaxes(held, 0, 1).reshape(full // wa_count, img_count, -1)
        held = jnp.roll(jnp.swapaxes(held, 0, 1), -lax.axis_index("img"), axis=0)
        total = add_up(held[0], *(shift(held[by], "img", by) for by in range(1, img_count)))
    blk = lax.axis_index("blk")
    total = total.reshape(2, total.shape[0] // 2, total.shape[1])
    mine = lax.dynamic_index_in_dim(total, blk, 0, keepdims=False)
    other = lax.dynamic_index_in_dim(total, 1 - blk, 0, keepdims=False)
    other = shift(other.astype(jnp.bfloat16), "blk", 1).astype(jnp.float32)
    count = mine.shape[1]
    source = jnp.arange(2 * count, dtype=jnp.int32)
    target = jnp.where(source < count, 2 * source + blk, 2 * (source - count) + 1 - blk)
    place = (target[:, None] == jnp.arange(2 * count, dtype=jnp.int32)[None, :]).astype(jnp.float32)
    both = jnp.concatenate([mine, other], axis=1)
    scale = 1.0 / math.sqrt(full * NV * planes * wa_count)
    return jnp.dot(both, place, precision=lax.Precision.HIGHEST) * scale


def solution(mesh):
    in_specs = (
        P(None, ("parts", "img"), "wa", "blk", None, None),
        P(("parts", "img"), "wa", "blk", None, None, None),
        P(("parts", "img"), "wa", "blk", None, None, None),
        P(("parts", "img"), "wa", "blk", None, None, None),
        P(("parts", "img"), "wa", "blk", None),
        P(("parts", "img"), "wa", "blk", None),
        P(("parts", "img"), "wa", "blk", None),
        P(("parts", "wa")),
    )
    out_specs = P(("parts", "wa", "blk"), "img")
    return jax.shard_map(shards, mesh=mesh, in_specs=in_specs, out_specs=out_specs, check_vma=False)
```

```python
import functools
import math

import jax
import jax.numpy as jnp
import numpy as np
from jax import lax
from jax.experimental import pallas as pl
from jax.experimental.pallas import tpu as pltpu
from jax.sharding import PartitionSpec as P

NV = 1024
LANES = 128
VMEM = pltpu.VMEM
SMEM = pltpu.SMEM
HBM = pltpu.HBM


def angles(first, second, length):
    return 2.0 * np.pi / length * (np.outer(first, second) % length)


def row_table(across, tile_width):
    half_v = np.arange(NV // 2)
    out = []
    for parity in range(2):
        m_index = 2 * np.arange(NV // 2) + parity
        ang = angles(half_v, m_index, NV)
        cosine, sine = np.cos(ang), np.sin(ang)
        real = np.stack([cosine, -sine])
        imag = np.stack([sine, cosine])
        both = np.stack([real, imag])
        both = both.reshape(2, 2, across // 2, tile_width, NV // 2 // LANES, LANES)
        out.append(both.transpose(4, 2, 1, 3, 0, 5).reshape(-1, NV, 2 * LANES))
    return np.stack(out)


def column_table(img_count, rows):
    full = img_count * rows
    ang = angles(np.arange(full // 2), np.arange(full), full)
    cosine, sine = np.cos(ang), np.sin(ang)
    sine[0] = np.cos(np.pi * (np.arange(full) % 2))
    both = np.stack([cosine, sine]).reshape(2, full // 2, img_count, rows)
    return both.transpose(2, 0, 1, 3)


def grid_kernel(
    counts_hbm,
    ids_hbm,
    planes_hbm,
    vis_hbm,
    mask_hbm,
    rk_hbm,
    ck_hbm,
    own_ref,
    send_ref,
    counts_ref,
    ids_ref,
    planes_ref,
    vis_ref,
    mask_ref,
    rk_ref,
    ck_ref,
    acc,
    small_sem,
    rk_sem,
    ck_sem,
):
    blk = lax.axis_index("blk")
    slots, rows, vis_len = rk_ref.shape
    codes = acc.shape[0]
    width = ck_ref.shape[2]
    blocks = mask_ref.shape[1]
    planes = own_ref.shape[0]
    across = codes // planes
    chunks = rk_sem.shape[0]
    group = slots // chunks

    small = [
        pltpu.make_async_copy(source, target, small_sem.at[n])
        for n, (source, target) in enumerate(
            [
                (counts_hbm, counts_ref),
                (ids_hbm, ids_ref),
                (planes_hbm, planes_ref),
                (vis_hbm, vis_ref),
                (mask_hbm, mask_ref),
            ]
        )
    ]
    large = []
    for n in range(chunks):
        part = pl.ds(n * group, group)
        large.append(
            [
                pltpu.make_async_copy(ck_hbm.at[part], ck_ref.at[part], ck_sem.at[n]),
                pltpu.make_async_copy(rk_hbm.at[part], rk_ref.at[part], rk_sem.at[n]),
            ]
        )
    for copy in small + sum(large, []):
        copy.start()
    acc[...] = jnp.zeros_like(acc)
    for copy in small:
        copy.wait()

    lane = lax.broadcasted_iota(jnp.int32, (1, vis_len), 1)
    real, imag = [], []
    for slot in range(slots):
        mask = mask_ref[slot].astype(jnp.float32) * (lane < counts_ref[slot]).astype(jnp.float32)
        real.append(mask * vis_ref[0, pl.ds(slot, 1), :].astype(jnp.float32))
        imag.append(mask * vis_ref[1, pl.ds(slot, 1), :].astype(jnp.float32))
    scaled = [jnp.concatenate(value, axis=0).T for value in (real, imag)]
    block_of = lax.broadcasted_iota(jnp.int32, (vis_len, width), 1) // (width // blocks)
    per = width // blocks
    for slot in range(slots):
        if slot % group == 0:
            for copy in large[slot // group]:
                copy.wait()
        here = slice(slot // per * width, (slot // per + 1) * width)
        source = block_of + slot % per * blocks
        weighted = jnp.concatenate(
            [
                jnp.take_along_axis(value[:, here], source, axis=1).astype(jnp.bfloat16)
                * ck_ref[slot]
                for value in scaled
            ],
            axis=1,
        )
        tile = jnp.dot(rk_ref[slot], weighted, preferred_element_type=jnp.float32)
        acc[planes_ref[slot] * across + ids_ref[slot]] += tile

    sign = (1 - 2 * blk).astype(jnp.float32)
    for plane in range(planes):
        for t in range(across // 2):
            low = acc[plane * across + t]
            high = acc[plane * across + t + across // 2] * sign
            where = pl.ds(t * 2 * width, 2 * width)
            own_ref[plane, :, where] = low + high
            send_ref[plane, :, where] = (low - high).astype(jnp.bfloat16)


def gridding(counts, ids, levels, vis, mask, rk, ck, planes):
    slots, rows, vis_len = rk.shape
    width = ck.shape[2]
    across = NV // width
    chunks = 4
    half = (planes, rows, NV)
    inputs = (counts, ids, levels, vis, mask, rk, ck)
    return pl.pallas_call(
        grid_kernel,
        in_specs=[pl.BlockSpec(memory_space=HBM)] * len(inputs),
        out_specs=[pl.BlockSpec(memory_space=VMEM)] * 2,
        out_shape=[
            jax.ShapeDtypeStruct(half, jnp.float32),
            jax.ShapeDtypeStruct(half, jnp.bfloat16),
        ],
        scratch_shapes=[SMEM(counts.shape, jnp.int32)] * 3
        + [VMEM(value.shape, value.dtype) for value in (vis, mask, rk, ck)]
        + [
            VMEM((planes * across, rows, 2 * width), jnp.float32),
            pltpu.SemaphoreType.DMA((5,)),
            pltpu.SemaphoreType.DMA((chunks,)),
            pltpu.SemaphoreType.DMA((chunks,)),
        ],
        compiler_params=pltpu.CompilerParams(vmem_limit_bytes=24 << 20),
        name="gridding",
    )(*(pltpu.with_memory_space_constraint(value, HBM) for value in inputs))


COS_POLY = np.polynomial.chebyshev.Chebyshev.interpolate(
    lambda z: np.cos(2 * np.pi * np.sqrt(np.maximum(z, 0.0))), 5, [0.0, 0.25]
).convert(kind=np.polynomial.Polynomial).coef
SIN_POLY = np.polynomial.chebyshev.Chebyshev.interpolate(
    lambda z: np.sinc(2 * np.sqrt(np.maximum(z, 0.0))) * 2 * np.pi, 5, [0.0, 0.25]
).convert(kind=np.polynomial.Polynomial).coef


def horner(coef, z):
    total = jnp.full_like(z, float(coef[-1]))
    for value in coef[-2::-1]:
        total = total * z + float(value)
    return total


def turn(cycles):
    rest = cycles - jnp.round(cycles)
    square = rest * rest
    return horner(COS_POLY, square), horner(SIN_POLY, square) * rest


def screen_kernel(
    w_ref, table_r_hbm, table_c_hbm, screen_ref, middle_ref, table_r_ref, table_c_ref, sem
):
    copies = [
        pltpu.make_async_copy(table_r_hbm.at[lax.axis_index("blk")], table_r_ref, sem.at[0]),
        pltpu.make_async_copy(table_c_hbm.at[lax.axis_index("img")], table_c_ref, sem.at[1]),
    ]
    for copy in copies:
        copy.start()
    planes, groups, half, _ = screen_ref.shape
    full = 2 * half
    blk = lax.axis_index("blk")
    block = LANES
    for g in range(groups):
        column = 2 * (g * LANES + lax.broadcasted_iota(jnp.int32, (1, LANES), 1)) + blk
        y = (column.astype(jnp.float32) - NV / 2) / NV
        rest_y = 1.0 - y * y
        for q in range(planes):
            cosine, sine = turn((jnp.sqrt(rest_y) - 1.0) * w_ref[q])
            middle_ref[q, g] = jnp.concatenate([cosine, sine], axis=1)
        for start in range(0, half, block):
            row = start + lax.broadcasted_iota(jnp.int32, (block, 1), 0)
            x = (row.astype(jnp.float32) - half) / full
            nterm = jnp.sqrt(rest_y - x * x) - 1.0
            for q in range(planes):
                cosine, sine = turn(nterm * w_ref[q])
                screen_ref[q, g, start : start + block, :LANES] = cosine
                screen_ref[q, g, start : start + block, LANES:] = sine
    for copy in copies:
        copy.wait()


def screens(w_values, table_r, table_c):
    planes = w_values.shape[0]
    groups = table_r.shape[1]
    half = table_c.shape[2]
    tables = [pltpu.with_memory_space_constraint(value, HBM) for value in (table_r, table_c)]
    return pl.pallas_call(
        screen_kernel,
        in_specs=[pl.BlockSpec(memory_space=SMEM)] + [pl.BlockSpec(memory_space=HBM)] * 2,
        out_specs=[pl.BlockSpec(memory_space=VMEM)] * 4,
        out_shape=[
            jax.ShapeDtypeStruct((planes, groups, half, 2 * LANES), jnp.float32),
            jax.ShapeDtypeStruct((planes, groups, 1, 2 * LANES), jnp.float32),
            jax.ShapeDtypeStruct(table_r.shape[1:], jnp.bfloat16),
            jax.ShapeDtypeStruct(table_c.shape[1:], jnp.bfloat16),
        ],
        scratch_shapes=[pltpu.SemaphoreType.DMA((2,))],
        compiler_params=pltpu.CompilerParams(vmem_limit_bytes=24 << 20),
        cost_estimate=pl.CostEstimate(
            flops=planes * half * NV * 20, bytes_accessed=planes * half * NV * 4, transcendentals=0
        ),
        name="screens",
    )(w_values, *tables)


def image_kernel(offsets, rotate, own_ref, recv_ref, table_r, table_c, screen_ref, middle_ref, *refs):
    outs, (rowdft, back) = refs[:-2], refs[-2:]
    planes, rows, _ = own_ref.shape
    groups = screen_ref.shape[1]
    grid = (own_ref[...] + recv_ref[...].astype(jnp.float32)).astype(jnp.bfloat16)
    grid = grid.reshape(planes * rows, NV)
    for g in range(groups):
        rowdft[g] = jnp.dot(grid, table_r[g], preferred_element_type=jnp.float32).astype(
            jnp.bfloat16
        )
    img = lax.axis_index("img")
    wa = lax.axis_index("wa")
    wa_count, piece = outs[0].shape[0], outs[0].shape[1]
    half = table_c.shape[1]
    block = LANES
    row_at = lax.broadcasted_iota(jnp.int32, (half, half), 0)
    col_at = lax.broadcasted_iota(jnp.int32, (half, half), 1)
    flip = (row_at == jnp.where(col_at == 0, 0, half - col_at)).astype(jnp.bfloat16)

    def put(start, count, n, value):
        for j in range(count // piece):
            at = lax.rem(start // piece + j - wa + wa_count, wa_count)
            outs[n][at] = value[j * piece : (j + 1) * piece]

    for n, k in enumerate(offsets):
        g = lax.rem(img + k, groups) if rotate else k
        firsts = []
        for start in range(0, half, block):
            even = jnp.zeros((block, LANES), jnp.float32)
            odd = jnp.zeros((block, LANES), jnp.float32)
            for q in range(planes):
                rhs = rowdft[g, q * rows : (q + 1) * rows]
                by_cos = jnp.dot(
                    table_c[0, start : start + block], rhs, preferred_element_type=jnp.float32
                )
                by_sin = jnp.dot(
                    table_c[1, start : start + block], rhs, preferred_element_type=jnp.float32
                )
                cosine = screen_ref[q, g, start : start + block, :LANES]
                sine = screen_ref[q, g, start : start + block, LANES:]
                even += cosine * by_cos[:, :LANES] - sine * by_cos[:, LANES:]
                if start == 0:
                    row = lax.broadcasted_iota(jnp.int32, (block, 1), 0)
                    cosine, sine = (
                        jnp.where(row == 0, -middle_ref[q, g, :, LANES:], cosine),
                        jnp.where(row == 0, middle_ref[q, g, :, :LANES], sine),
                    )
                odd += cosine * by_sin[:, LANES:] + sine * by_sin[:, :LANES]
            low, high = even - odd, even + odd
            if start == 0:
                low = jnp.where(row == 0, even, low)
                high = jnp.where(row == 0, odd, high)
            firsts.append(low.astype(jnp.bfloat16))
            back[start : start + block] = high.astype(jnp.bfloat16)
        put(0, half, n, jnp.concatenate(firsts, axis=0))
        second = jnp.dot(flip, back[...], preferred_element_type=jnp.float32).astype(jnp.bfloat16)
        put(half, half, n, second)


def images(offsets, rotate, wa_count, own, recv, screen, middle, table_r, table_c):
    half = table_c.shape[1]
    planes, rows, _ = own.shape
    inputs = (own, recv, table_r, table_c, screen, middle)
    one = jax.ShapeDtypeStruct((wa_count, 2 * half // wa_count, LANES), jnp.bfloat16)
    return pl.pallas_call(
        functools.partial(image_kernel, offsets, rotate),
        in_specs=[pl.BlockSpec(memory_space=VMEM)] * len(inputs),
        out_specs=[pl.BlockSpec(memory_space=VMEM)] * len(offsets),
        out_shape=[one] * len(offsets),
        scratch_shapes=[
            VMEM((table_r.shape[0], planes * rows, 2 * LANES), jnp.bfloat16),
            VMEM((half, LANES), jnp.bfloat16),
        ],
        compiler_params=pltpu.CompilerParams(vmem_limit_bytes=24 << 20),
        name="image",
    )(*inputs)


def add_kernel(one_ref, *refs):
    total = one_ref[...].astype(jnp.float32)
    for ref in refs[:-1]:
        total += ref[...].astype(jnp.float32)
    refs[-1][...] = total.astype(refs[-1].dtype)


def add_rounded(*parts):
    return pl.pallas_call(
        add_kernel,
        in_specs=[pl.BlockSpec(memory_space=VMEM)] * len(parts),
        out_specs=pl.BlockSpec(memory_space=VMEM),
        out_shape=jax.ShapeDtypeStruct(parts[0].shape, jnp.bfloat16),
        compiler_params=pltpu.CompilerParams(vmem_limit_bytes=24 << 20),
        name="add",
    )(*parts)


def add_up(*parts):
    return sum(part.astype(jnp.float32) for part in parts)


def final_kernel(scale, mine_ref, other_ref, out_ref):
    blk = lax.axis_index("blk")
    count = mine_ref.shape[1]
    source = lax.broadcasted_iota(jnp.int32, (2 * count, 2 * count), 0)
    target = lax.broadcasted_iota(jnp.int32, (2 * count, 2 * count), 1)
    wanted = jnp.where(source < count, 2 * source + blk, 2 * (source - count) + 1 - blk)
    place = (wanted == target).astype(jnp.bfloat16)
    rest = jnp.concatenate([mine_ref[...], other_ref[...].astype(jnp.float32)], axis=1) * scale
    total = jnp.zeros(out_ref.shape, jnp.float32)
    for _ in range(3):
        term = rest.astype(jnp.bfloat16)
        total += jnp.dot(term, place, preferred_element_type=jnp.float32)
        rest = rest - term.astype(jnp.float32)
    out_ref[...] = total


def interleave(mine, other, scale):
    return pl.pallas_call(
        functools.partial(final_kernel, scale),
        in_specs=[pl.BlockSpec(memory_space=VMEM)] * 2,
        out_specs=pl.BlockSpec(memory_space=VMEM),
        out_shape=jax.ShapeDtypeStruct((mine.shape[0], 2 * mine.shape[1]), jnp.float32),
        compiler_params=pltpu.CompilerParams(vmem_limit_bytes=24 << 20),
        name="interleave",
    )(mine, other)


def shift(value, axis, by):
    count = lax.axis_size(axis)
    return lax.ppermute(value, axis, [(one, (one + by) % count) for one in range(count)])


def shards(
    visibilities, row_kernel, col_kernel, block_mask, tile_counts, tile_ids, tile_planes, w_values
):
    slots = tile_counts.shape[3]
    planes = w_values.shape[0]
    rows, vis_len = row_kernel.shape[4], row_kernel.shape[5]
    width = col_kernel.shape[5]
    img_count = lax.axis_size("img")
    wa_count = lax.axis_size("wa")
    full = rows * img_count
    table_r = jnp.asarray(row_table(NV // width, width), jnp.bfloat16)
    table_c = jnp.asarray(column_table(img_count, rows), jnp.bfloat16)
    own, send = gridding(
        tile_counts.reshape(slots),
        tile_ids.reshape(slots),
        tile_planes.reshape(slots),
        visibilities.reshape(2, slots, vis_len),
        block_mask.reshape(slots, -1, vis_len),
        row_kernel.reshape(slots, rows, vis_len),
        col_kernel.reshape(slots, vis_len, width),
        planes,
    )
    recv = shift(send, "blk", 1)
    screen, middle, table_r, table_c = screens(w_values, table_r, table_c)
    groups = screen.shape[1]
    rotate = groups == img_count
    offsets = [2, 3, 1, 0] if rotate else list(range(groups))
    parts = images(
        offsets, rotate, wa_count, own, recv, screen, middle, table_r, table_c
    )

    def over_wa(part):
        return [shift(part[by], "wa", by) for by in range(1, wa_count)]

    if rotate:
        far, before, after, here = parts
        from_after = shift(before, "img", 3)
        far = add_rounded(far[0], *over_wa(far))
        after = add_rounded(after[0], *over_wa(after))
        from_far = shift(far, "img", 2)
        from_before = shift(after, "img", 1)
        here = add_rounded(here, from_after)
        total = add_up(here[0], *over_wa(here), from_far, from_before)
    else:
        part = jnp.stack(parts, axis=1)
        held = add_rounded(part[0], *over_wa(part))
        held = jnp.swapaxes(held, 0, 1).reshape(full // wa_count, img_count, -1)
        held = jnp.roll(jnp.swapaxes(held, 0, 1), -lax.axis_index("img"), axis=0)
        total = add_up(held[0], *(shift(held[by], "img", by) for by in range(1, img_count)))
    blk = lax.axis_index("blk")
    total = total.reshape(2, total.shape[0] // 2, total.shape[1])
    mine = lax.dynamic_index_in_dim(total, blk, 0, keepdims=False)
    other = lax.dynamic_index_in_dim(total, 1 - blk, 0, keepdims=False)
    other = shift(other.astype(jnp.bfloat16), "blk", 1)
    return interleave(mine, other, 1.0 / math.sqrt(full * NV * planes * wa_count))


def solution(mesh):
    in_specs = (
        P(None, ("parts", "img"), "wa", "blk", None, None),
        P(("parts", "img"), "wa", "blk", None, None, None),
        P(("parts", "img"), "wa", "blk", None, None, None),
        P(("parts", "img"), "wa", "blk", None, None, None),
        P(("parts", "img"), "wa", "blk", None),
        P(("parts", "img"), "wa", "blk", None),
        P(("parts", "img"), "wa", "blk", None),
        P(("parts", "wa")),
    )
    out_specs = P(("parts", "wa", "blk"), "img")
    return jax.shard_map(shards, mesh=mesh, in_specs=in_specs, out_specs=out_specs, check_vma=False)
```

```python
import functools
import math

import jax
import jax.numpy as jnp
import numpy as np
from jax import lax
from jax.experimental import pallas as pl
from jax.experimental.pallas import tpu as pltpu
from jax.sharding import PartitionSpec as P

NV = 1024
LANES = 128
VMEM = pltpu.VMEM
SMEM = pltpu.SMEM
HBM = pltpu.HBM


def angles(first, second, length):
    return 2.0 * np.pi / length * (np.outer(first, second) % length)


def row_table(across, tile_width):
    half_v = np.arange(NV // 2)
    out = []
    for parity in range(2):
        m_index = 2 * np.arange(NV // 2) + parity
        ang = angles(half_v, m_index, NV)
        cosine, sine = np.cos(ang), np.sin(ang)
        real = np.stack([cosine, -sine])
        imag = np.stack([sine, cosine])
        both = np.stack([real, imag])
        both = both.reshape(2, 2, across // 2, tile_width, NV // 2 // LANES, LANES)
        out.append(both.transpose(4, 2, 1, 3, 0, 5).reshape(-1, NV, 2 * LANES))
    return np.stack(out)


def column_table(img_count, rows):
    full = img_count * rows
    ang = angles(np.arange(full // 2), np.arange(full), full)
    cosine, sine = np.cos(ang), np.sin(ang)
    sine[0] = np.cos(np.pi * (np.arange(full) % 2))
    both = np.stack([cosine, sine]).reshape(2, full // 2, img_count, rows)
    return both.transpose(2, 0, 1, 3)


def grid_kernel(
    counts_hbm,
    ids_hbm,
    planes_hbm,
    vis_hbm,
    mask_hbm,
    rk_hbm,
    ck_hbm,
    own_ref,
    send_ref,
    counts_ref,
    ids_ref,
    planes_ref,
    vis_ref,
    mask_ref,
    rk_ref,
    ck_ref,
    acc,
    small_sem,
    rk_sem,
    ck_sem,
):
    blk = lax.axis_index("blk")
    slots, rows, vis_len = rk_ref.shape
    codes = acc.shape[0]
    width = ck_ref.shape[2]
    blocks = mask_ref.shape[1]
    planes = own_ref.shape[0]
    across = codes // planes
    chunks = rk_sem.shape[0]
    group = slots // chunks

    small = [
        pltpu.make_async_copy(source, target, small_sem.at[n])
        for n, (source, target) in enumerate(
            [
                (counts_hbm, counts_ref),
                (ids_hbm, ids_ref),
                (planes_hbm, planes_ref),
                (vis_hbm, vis_ref),
                (mask_hbm, mask_ref),
            ]
        )
    ]
    large = []
    for n in range(chunks):
        part = pl.ds(n * group, group)
        large.append(
            [
                pltpu.make_async_copy(ck_hbm.at[part], ck_ref.at[part], ck_sem.at[n]),
                pltpu.make_async_copy(rk_hbm.at[part], rk_ref.at[part], rk_sem.at[n]),
            ]
        )
    for copy in small + sum(large, []):
        copy.start()
    acc[...] = jnp.zeros_like(acc)
    for copy in small:
        copy.wait()

    lane = lax.broadcasted_iota(jnp.int32, (1, vis_len), 1)
    real, imag = [], []
    for slot in range(slots):
        mask = mask_ref[slot].astype(jnp.float32) * (lane < counts_ref[slot]).astype(jnp.float32)
        real.append(mask * vis_ref[0, pl.ds(slot, 1), :].astype(jnp.float32))
        imag.append(mask * vis_ref[1, pl.ds(slot, 1), :].astype(jnp.float32))
    scaled = [jnp.concatenate(value, axis=0).T for value in (real, imag)]
    block_of = lax.broadcasted_iota(jnp.int32, (vis_len, width), 1) // (width // blocks)
    per = width // blocks
    for slot in range(slots):
        if slot % group == 0:
            for copy in large[slot // group]:
                copy.wait()
        here = slice(slot // per * width, (slot // per + 1) * width)
        source = block_of + slot % per * blocks
        weighted = jnp.concatenate(
            [
                jnp.take_along_axis(value[:, here], source, axis=1).astype(jnp.bfloat16)
                * ck_ref[slot]
                for value in scaled
            ],
            axis=1,
        )
        tile = jnp.dot(rk_ref[slot], weighted, preferred_element_type=jnp.float32)
        acc[planes_ref[slot] * across + ids_ref[slot]] += tile

    sign = (1 - 2 * blk).astype(jnp.float32)
    for plane in range(planes):
        for t in range(across // 2):
            low = acc[plane * across + t]
            high = acc[plane * across + t + across // 2] * sign
            where = pl.ds(t * 2 * width, 2 * width)
            own_ref[plane, :, where] = low + high
            send_ref[plane, :, where] = (low - high).astype(jnp.bfloat16)


def gridding(counts, ids, levels, vis, mask, rk, ck, planes):
    slots, rows, vis_len = rk.shape
    width = ck.shape[2]
    across = NV // width
    chunks = 4
    half = (planes, rows, NV)
    inputs = (counts, ids, levels, vis, mask, rk, ck)
    return pl.pallas_call(
        grid_kernel,
        in_specs=[pl.BlockSpec(memory_space=HBM)] * len(inputs),
        out_specs=[pl.BlockSpec(memory_space=VMEM)] * 2,
        out_shape=[
            jax.ShapeDtypeStruct(half, jnp.float32),
            jax.ShapeDtypeStruct(half, jnp.bfloat16),
        ],
        scratch_shapes=[SMEM(counts.shape, jnp.int32)] * 3
        + [VMEM(value.shape, value.dtype) for value in (vis, mask, rk, ck)]
        + [
            VMEM((planes * across, rows, 2 * width), jnp.float32),
            pltpu.SemaphoreType.DMA((5,)),
            pltpu.SemaphoreType.DMA((chunks,)),
            pltpu.SemaphoreType.DMA((chunks,)),
        ],
        compiler_params=pltpu.CompilerParams(vmem_limit_bytes=24 << 20),
        name="gridding",
    )(*(pltpu.with_memory_space_constraint(value, HBM) for value in inputs))


COS_POLY = np.polynomial.chebyshev.Chebyshev.interpolate(
    lambda z: np.cos(2 * np.pi * np.sqrt(np.maximum(z, 0.0))), 5, [0.0, 0.25]
).convert(kind=np.polynomial.Polynomial).coef
SIN_POLY = np.polynomial.chebyshev.Chebyshev.interpolate(
    lambda z: np.sinc(2 * np.sqrt(np.maximum(z, 0.0))) * 2 * np.pi, 5, [0.0, 0.25]
).convert(kind=np.polynomial.Polynomial).coef


def horner(coef, z):
    total = jnp.full_like(z, float(coef[-1]))
    for value in coef[-2::-1]:
        total = total * z + float(value)
    return total


def turn(cycles):
    rest = cycles - jnp.round(cycles)
    square = rest * rest
    return horner(COS_POLY, square), horner(SIN_POLY, square) * rest


def screen_kernel(
    w_ref, table_r_hbm, table_c_hbm, screen_ref, middle_ref, table_r_ref, *refs
):
    columns, sem = refs[:-1], refs[-1]
    img = lax.axis_index("img")
    copies = [pltpu.make_async_copy(table_r_hbm.at[lax.axis_index("blk")], table_r_ref, sem.at[0])]
    for n, ref in enumerate(columns):
        source = table_c_hbm.at[img ^ n]
        copies.append(pltpu.make_async_copy(source, ref, sem.at[1 + n]))
    for copy in copies:
        copy.start()
    planes, groups, half, _ = screen_ref.shape
    full = 2 * half
    blk = lax.axis_index("blk")
    block = LANES
    for g in range(groups):
        column = 2 * (g * LANES + lax.broadcasted_iota(jnp.int32, (1, LANES), 1)) + blk
        y = (column.astype(jnp.float32) - NV / 2) / NV
        rest_y = 1.0 - y * y
        for q in range(planes):
            cosine, sine = turn((jnp.sqrt(rest_y) - 1.0) * w_ref[q])
            middle_ref[q, g] = jnp.concatenate([cosine, sine], axis=1)
        for start in range(0, half, block):
            row = start + lax.broadcasted_iota(jnp.int32, (block, 1), 0)
            x = (row.astype(jnp.float32) - half) / full
            nterm = jnp.sqrt(rest_y - x * x) - 1.0
            for q in range(planes):
                cosine, sine = turn(nterm * w_ref[q])
                screen_ref[q, g, start : start + block, :LANES] = cosine
                screen_ref[q, g, start : start + block, LANES:] = sine
    for copy in copies:
        copy.wait()


def screens(w_values, table_r, table_c, n_columns):
    planes = w_values.shape[0]
    groups = table_r.shape[1]
    half = table_c.shape[2]
    tables = [pltpu.with_memory_space_constraint(value, HBM) for value in (table_r, table_c)]
    return pl.pallas_call(
        screen_kernel,
        in_specs=[pl.BlockSpec(memory_space=SMEM)] + [pl.BlockSpec(memory_space=HBM)] * 2,
        out_specs=[pl.BlockSpec(memory_space=VMEM)] * (3 + n_columns),
        out_shape=[
            jax.ShapeDtypeStruct((planes, groups, half, 2 * LANES), jnp.float32),
            jax.ShapeDtypeStruct((planes, groups, 1, 2 * LANES), jnp.float32),
            jax.ShapeDtypeStruct(table_r.shape[1:], jnp.bfloat16),
        ]
        + [jax.ShapeDtypeStruct(table_c.shape[1:], jnp.bfloat16)] * n_columns,
        scratch_shapes=[pltpu.SemaphoreType.DMA((1 + n_columns,))],
        compiler_params=pltpu.CompilerParams(vmem_limit_bytes=24 << 20),
        cost_estimate=pl.CostEstimate(
            flops=planes * half * NV * 20, bytes_accessed=planes * half * NV * 4, transcendentals=0
        ),
        name="screens",
    )(w_values, *tables)


def row_kernel_body(offsets, rotate, own_ref, recv_ref, table_r, *outs):
    planes, rows, _ = own_ref.shape
    groups = table_r.shape[0]
    grid = (own_ref[...] + recv_ref[...].astype(jnp.float32)).astype(jnp.bfloat16)
    grid = grid.reshape(planes * rows, NV)
    for out_ref, k in zip(outs, offsets):
        g = lax.axis_index("img") ^ k if rotate else k
        out_ref[...] = jnp.dot(grid, table_r[g], preferred_element_type=jnp.float32).astype(
            jnp.bfloat16
        )


def row_transform(offsets, rotate, own, recv, table_r):
    planes, rows, _ = own.shape
    one = jax.ShapeDtypeStruct((planes * rows, 2 * LANES), jnp.bfloat16)
    return pl.pallas_call(
        functools.partial(row_kernel_body, offsets, rotate),
        in_specs=[pl.BlockSpec(memory_space=VMEM)] * 3,
        out_specs=[pl.BlockSpec(memory_space=VMEM)] * len(offsets),
        out_shape=[one] * len(offsets),
        compiler_params=pltpu.CompilerParams(vmem_limit_bytes=24 << 20),
        name="row_dft",
    )(own, recv, table_r)


def image_kernel(offsets, rotate, depth, *refs):
    rowdft = refs[: len(offsets) * depth]
    tables = refs[len(offsets) * depth : (len(offsets) + 1) * depth]
    screen_ref, middle_ref, *outs, back = refs[(len(offsets) + 1) * depth :]
    planes, groups = screen_ref.shape[:2]
    rows = rowdft[0].shape[0] // planes
    img = lax.axis_index("img")
    wa = lax.axis_index("wa")
    wa_count, piece = outs[0].shape[0], outs[0].shape[1]
    half = tables[0].shape[1]
    block = LANES
    row_at = lax.broadcasted_iota(jnp.int32, (half, half), 0)
    col_at = lax.broadcasted_iota(jnp.int32, (half, half), 1)
    flip = (row_at == jnp.where(col_at == 0, 0, half - col_at)).astype(jnp.bfloat16)

    def put(start, count, n, value):
        for j in range(count // piece):
            at = lax.rem(start // piece + j - wa + wa_count, wa_count)
            outs[n][at] = value[j * piece : (j + 1) * piece]

    for n, k in enumerate(offsets):
        g = img ^ k if rotate else k
        firsts = []
        for start in range(0, half, block):
            even = jnp.zeros((block, LANES), jnp.float32)
            odd = jnp.zeros((block, LANES), jnp.float32)
            for q in range(planes):
                by_cos, by_sin = (
                    sum(
                        jnp.dot(
                            tables[d][which, start : start + block],
                            rowdft[n * depth + d][q * rows : (q + 1) * rows],
                            preferred_element_type=jnp.float32,
                        )
                        for d in range(depth)
                    )
                    for which in range(2)
                )
                cosine = screen_ref[q, g, start : start + block, :LANES]
                sine = screen_ref[q, g, start : start + block, LANES:]
                even += cosine * by_cos[:, :LANES] - sine * by_cos[:, LANES:]
                if start == 0:
                    row = lax.broadcasted_iota(jnp.int32, (block, 1), 0)
                    cosine, sine = (
                        jnp.where(row == 0, -middle_ref[q, g, :, LANES:], cosine),
                        jnp.where(row == 0, middle_ref[q, g, :, :LANES], sine),
                    )
                odd += cosine * by_sin[:, LANES:] + sine * by_sin[:, :LANES]
            low, high = even - odd, even + odd
            if start == 0:
                low = jnp.where(row == 0, even, low)
                high = jnp.where(row == 0, odd, high)
            firsts.append(low.astype(jnp.bfloat16))
            back[start : start + block] = high.astype(jnp.bfloat16)
        put(0, half, n, jnp.concatenate(firsts, axis=0))
        second = jnp.dot(flip, back[...], preferred_element_type=jnp.float32).astype(jnp.bfloat16)
        put(half, half, n, second)


def images(offsets, rotate, wa_count, rowdft, tables, screen, middle):
    half = tables[0].shape[1]
    inputs = (*rowdft, *tables, screen, middle)
    one = jax.ShapeDtypeStruct((wa_count, 2 * half // wa_count, LANES), jnp.bfloat16)
    return pl.pallas_call(
        functools.partial(image_kernel, offsets, rotate, len(tables)),
        in_specs=[pl.BlockSpec(memory_space=VMEM)] * len(inputs),
        out_specs=[pl.BlockSpec(memory_space=VMEM)] * len(offsets),
        out_shape=[one] * len(offsets),
        scratch_shapes=[VMEM((half, LANES), jnp.bfloat16)],
        compiler_params=pltpu.CompilerParams(vmem_limit_bytes=24 << 20),
        name="image" + "".join(str(k) for k in offsets),
    )(*inputs)


def add_kernel(one_ref, *refs):
    total = one_ref[...].astype(jnp.float32)
    for ref in refs[:-1]:
        total += ref[...].astype(jnp.float32)
    refs[-1][...] = total.astype(refs[-1].dtype)


def add_rounded(*parts):
    return pl.pallas_call(
        add_kernel,
        in_specs=[pl.BlockSpec(memory_space=VMEM)] * len(parts),
        out_specs=pl.BlockSpec(memory_space=VMEM),
        out_shape=jax.ShapeDtypeStruct(parts[0].shape, jnp.bfloat16),
        compiler_params=pltpu.CompilerParams(vmem_limit_bytes=24 << 20),
        name="add",
    )(*parts)


def add_up(*parts):
    return sum(part.astype(jnp.float32) for part in parts)


def final_kernel(scale, mine_ref, other_ref, out_ref):
    blk = lax.axis_index("blk")
    count = mine_ref.shape[1]
    source = lax.broadcasted_iota(jnp.int32, (2 * count, 2 * count), 0)
    target = lax.broadcasted_iota(jnp.int32, (2 * count, 2 * count), 1)
    wanted = jnp.where(source < count, 2 * source + blk, 2 * (source - count) + 1 - blk)
    place = (wanted == target).astype(jnp.bfloat16)
    rest = jnp.concatenate([mine_ref[...], other_ref[...].astype(jnp.float32)], axis=1) * scale
    total = jnp.zeros(out_ref.shape, jnp.float32)
    for _ in range(3):
        term = rest.astype(jnp.bfloat16)
        total += jnp.dot(term, place, preferred_element_type=jnp.float32)
        rest = rest - term.astype(jnp.float32)
    out_ref[...] = total


def interleave(mine, other, scale):
    return pl.pallas_call(
        functools.partial(final_kernel, scale),
        in_specs=[pl.BlockSpec(memory_space=VMEM)] * 2,
        out_specs=pl.BlockSpec(memory_space=VMEM),
        out_shape=jax.ShapeDtypeStruct((mine.shape[0], 2 * mine.shape[1]), jnp.float32),
        compiler_params=pltpu.CompilerParams(vmem_limit_bytes=24 << 20),
        name="interleave",
    )(mine, other)


def shift(value, axis, by):
    count = lax.axis_size(axis)
    return lax.ppermute(value, axis, [(one, (one + by) % count) for one in range(count)])


def swap(value, axis, bits):
    count = lax.axis_size(axis)
    return lax.ppermute(value, axis, [(one, one ^ bits) for one in range(count)])


def shards(
    visibilities, row_kernel, col_kernel, block_mask, tile_counts, tile_ids, tile_planes, w_values
):
    slots = tile_counts.shape[3]
    planes = w_values.shape[0]
    rows, vis_len = row_kernel.shape[4], row_kernel.shape[5]
    width = col_kernel.shape[5]
    img_count = lax.axis_size("img")
    wa_count = lax.axis_size("wa")
    full = rows * img_count
    table_r = jnp.asarray(row_table(NV // width, width), jnp.bfloat16)
    table_c = jnp.asarray(column_table(img_count, rows), jnp.bfloat16)
    own, send = gridding(
        tile_counts.reshape(slots),
        tile_ids.reshape(slots),
        tile_planes.reshape(slots),
        visibilities.reshape(2, slots, vis_len),
        block_mask.reshape(slots, -1, vis_len),
        row_kernel.reshape(slots, rows, vis_len),
        col_kernel.reshape(slots, vis_len, width),
        planes,
    )
    recv = shift(send, "blk", 1)
    groups = NV // 2 // LANES
    rotate = groups == img_count
    offsets = [1, 3, 2, 0] if rotate else list(range(groups))
    screen, middle, table_r, *columns = screens(w_values, table_r, table_c, 2 if rotate else 1)
    rowdft = row_transform(offsets, rotate, own, recv, table_r)

    def over_wa(part):
        return [shift(part[by], "wa", by) for by in range(1, wa_count)]

    if rotate:
        beside, outer, far, here = rowdft
        from_beside = swap(beside, "img", 1)
        outer, far = images([3, 2], rotate, wa_count, [outer, far], columns[:1], screen, middle)
        outer = add_rounded(outer[0], *over_wa(outer))
        far = add_rounded(far[0], *over_wa(far))
        from_outer = swap(outer, "img", 3)
        from_far = swap(far, "img", 2)
        (here,) = images([0], rotate, wa_count, [here, from_beside], columns, screen, middle)
        total = add_up(here[0], *over_wa(here), from_outer, from_far)
    else:
        parts = images(offsets, rotate, wa_count, rowdft, columns, screen, middle)
        part = jnp.stack(parts, axis=1)
        held = add_rounded(part[0], *over_wa(part))
        held = jnp.swapaxes(held, 0, 1).reshape(full // wa_count, img_count, -1)
        held = jnp.roll(jnp.swapaxes(held, 0, 1), -lax.axis_index("img"), axis=0)
        total = add_up(held[0], *(shift(held[by], "img", by) for by in range(1, img_count)))
    blk = lax.axis_index("blk")
    total = total.reshape(2, total.shape[0] // 2, total.shape[1])
    mine = lax.dynamic_index_in_dim(total, blk, 0, keepdims=False)
    other = lax.dynamic_index_in_dim(total, 1 - blk, 0, keepdims=False)
    other = shift(other.astype(jnp.bfloat16), "blk", 1)
    return interleave(mine, other, 1.0 / math.sqrt(full * NV * planes * wa_count))


def solution(mesh):
    in_specs = (
        P(None, ("parts", "img"), "wa", "blk", None, None),
        P(("parts", "img"), "wa", "blk", None, None, None),
        P(("parts", "img"), "wa", "blk", None, None, None),
        P(("parts", "img"), "wa", "blk", None, None, None),
        P(("parts", "img"), "wa", "blk", None),
        P(("parts", "img"), "wa", "blk", None),
        P(("parts", "img"), "wa", "blk", None),
        P(("parts", "wa")),
    )
    out_specs = P(("parts", "wa", "blk"), "img")
    return jax.shard_map(shards, mesh=mesh, in_specs=in_specs, out_specs=out_specs, check_vma=False)
```

```python
import functools
import math

import jax
import jax.numpy as jnp
import numpy as np
from jax import lax
from jax.experimental import pallas as pl
from jax.experimental.pallas import tpu as pltpu
from jax.sharding import PartitionSpec as P

NV = 1024
LANES = 128
VMEM = pltpu.VMEM
SMEM = pltpu.SMEM
HBM = pltpu.HBM


def angles(first, second, length):
    return 2.0 * np.pi / length * (np.outer(first, second) % length)


def row_table(across, tile_width):
    half_v = np.arange(NV // 2)
    out = []
    for parity in range(2):
        m_index = 2 * np.arange(NV // 2) + parity
        ang = angles(half_v, m_index, NV)
        cosine, sine = np.cos(ang), np.sin(ang)
        real = np.stack([cosine, -sine])
        imag = np.stack([sine, cosine])
        both = np.stack([real, imag])
        both = both.reshape(2, 2, across // 2, tile_width, NV // 2 // LANES, LANES)
        out.append(both.transpose(4, 2, 1, 3, 0, 5).reshape(-1, NV, 2 * LANES))
    return np.stack(out)


def column_table(img_count, rows):
    full = img_count * rows
    ang = angles(np.arange(full // 2), np.arange(full), full)
    cosine, sine = np.cos(ang), np.sin(ang)
    sine[0] = np.cos(np.pi * (np.arange(full) % 2))
    both = np.stack([cosine, sine]).reshape(2, full // 2, img_count, rows)
    return both.transpose(2, 0, 1, 3)


def grid_kernel(
    counts_hbm,
    ids_hbm,
    planes_hbm,
    vis_hbm,
    mask_hbm,
    rk_hbm,
    ck_hbm,
    own_ref,
    send_ref,
    counts_ref,
    ids_ref,
    planes_ref,
    vis_ref,
    mask_ref,
    rk_ref,
    ck_ref,
    acc,
    small_sem,
    rk_sem,
    ck_sem,
):
    blk = lax.axis_index("blk")
    slots, rows, vis_len = rk_ref.shape
    codes = acc.shape[0]
    width = ck_ref.shape[2]
    blocks = mask_ref.shape[1]
    planes = own_ref.shape[0]
    across = codes // planes
    chunks = rk_sem.shape[0]
    group = slots // chunks

    small = [
        pltpu.make_async_copy(source, target, small_sem.at[n])
        for n, (source, target) in enumerate(
            [
                (counts_hbm, counts_ref),
                (ids_hbm, ids_ref),
                (planes_hbm, planes_ref),
                (vis_hbm, vis_ref),
                (mask_hbm, mask_ref),
            ]
        )
    ]
    large = []
    for n in range(chunks):
        part = pl.ds(n * group, group)
        large.append(
            [
                pltpu.make_async_copy(ck_hbm.at[part], ck_ref.at[part], ck_sem.at[n]),
                pltpu.make_async_copy(rk_hbm.at[part], rk_ref.at[part], rk_sem.at[n]),
            ]
        )
    for copy in small + sum(large, []):
        copy.start()
    acc[...] = jnp.zeros_like(acc)
    for copy in small:
        copy.wait()

    lane = lax.broadcasted_iota(jnp.int32, (1, vis_len), 1)
    real, imag = [], []
    for slot in range(slots):
        mask = mask_ref[slot].astype(jnp.float32) * (lane < counts_ref[slot]).astype(jnp.float32)
        real.append(mask * vis_ref[0, pl.ds(slot, 1), :].astype(jnp.float32))
        imag.append(mask * vis_ref[1, pl.ds(slot, 1), :].astype(jnp.float32))
    scaled = [jnp.concatenate(value, axis=0).T for value in (real, imag)]
    block_of = lax.broadcasted_iota(jnp.int32, (vis_len, width), 1) // (width // blocks)
    per = width // blocks
    for slot in range(slots):
        if slot % group == 0:
            for copy in large[slot // group]:
                copy.wait()
        here = slice(slot // per * width, (slot // per + 1) * width)
        source = block_of + slot % per * blocks
        weighted = jnp.concatenate(
            [
                jnp.take_along_axis(value[:, here], source, axis=1).astype(jnp.bfloat16)
                * ck_ref[slot]
                for value in scaled
            ],
            axis=1,
        )
        tile = jnp.dot(rk_ref[slot], weighted, preferred_element_type=jnp.float32)
        acc[planes_ref[slot] * across + ids_ref[slot]] += tile

    sign = (1 - 2 * blk).astype(jnp.float32)
    for plane in range(planes):
        for t in range(across // 2):
            low = acc[plane * across + t]
            high = acc[plane * across + t + across // 2] * sign
            where = pl.ds(t * 2 * width, 2 * width)
            own_ref[plane, :, where] = low + high
            send_ref[plane, :, where] = (low - high).astype(jnp.bfloat16)


def gridding(counts, ids, levels, vis, mask, rk, ck, planes):
    slots, rows, vis_len = rk.shape
    width = ck.shape[2]
    across = NV // width
    chunks = 2
    half = (planes, rows, NV)
    inputs = (counts, ids, levels, vis, mask, rk, ck)
    return pl.pallas_call(
        grid_kernel,
        in_specs=[pl.BlockSpec(memory_space=HBM)] * len(inputs),
        out_specs=[pl.BlockSpec(memory_space=VMEM)] * 2,
        out_shape=[
            jax.ShapeDtypeStruct(half, jnp.float32),
            jax.ShapeDtypeStruct(half, jnp.bfloat16),
        ],
        scratch_shapes=[SMEM(counts.shape, jnp.int32)] * 3
        + [VMEM(value.shape, value.dtype) for value in (vis, mask, rk, ck)]
        + [
            VMEM((planes * across, rows, 2 * width), jnp.float32),
            pltpu.SemaphoreType.DMA((5,)),
            pltpu.SemaphoreType.DMA((chunks,)),
            pltpu.SemaphoreType.DMA((chunks,)),
        ],
        compiler_params=pltpu.CompilerParams(vmem_limit_bytes=24 << 20),
        name="gridding",
    )(*(pltpu.with_memory_space_constraint(value, HBM) for value in inputs))


COS_POLY = np.polynomial.chebyshev.Chebyshev.interpolate(
    lambda z: np.cos(2 * np.pi * np.sqrt(np.maximum(z, 0.0))), 5, [0.0, 0.25]
).convert(kind=np.polynomial.Polynomial).coef
SIN_POLY = np.polynomial.chebyshev.Chebyshev.interpolate(
    lambda z: np.sinc(2 * np.sqrt(np.maximum(z, 0.0))) * 2 * np.pi, 5, [0.0, 0.25]
).convert(kind=np.polynomial.Polynomial).coef


def horner(coef, z):
    total = jnp.full_like(z, float(coef[-1]))
    for value in coef[-2::-1]:
        total = total * z + float(value)
    return total


def turn(cycles):
    rest = cycles - jnp.round(cycles)
    square = rest * rest
    return horner(COS_POLY, square), horner(SIN_POLY, square) * rest


def screen_kernel(
    offsets, neighbours, rotate, w_ref, table_r_hbm, table_c_hbm, screen_ref, middle_ref, table_r_ref, *refs
):
    columns, sem = refs[:-1], refs[-1]
    img = lax.axis_index("img")
    copies = [pltpu.make_async_copy(table_r_hbm.at[lax.axis_index("blk")], table_r_ref, sem.at[0])]
    for n, ref in enumerate(columns):
        source = table_c_hbm.at[img ^ neighbours[n]]
        copies.append(pltpu.make_async_copy(source, ref, sem.at[1 + n]))
    for copy in copies:
        copy.start()
    planes, _, half, _ = screen_ref.shape
    full = 2 * half
    blk = lax.axis_index("blk")
    block = LANES
    for n, k in enumerate(offsets):
        g = lax.axis_index("img") ^ k if rotate else k
        column = 2 * (g * LANES + lax.broadcasted_iota(jnp.int32, (1, LANES), 1)) + blk
        y = (column.astype(jnp.float32) - NV / 2) / NV
        rest_y = 1.0 - y * y
        for q in range(planes):
            cosine, sine = turn((jnp.sqrt(rest_y) - 1.0) * w_ref[q])
            middle_ref[q, n] = jnp.concatenate([cosine, sine], axis=1)
        for start in range(0, half, block):
            row = start + lax.broadcasted_iota(jnp.int32, (block, 1), 0)
            x = (row.astype(jnp.float32) - half) / full
            nterm = jnp.sqrt(rest_y - x * x) - 1.0
            for q in range(planes):
                cosine, sine = turn(nterm * w_ref[q])
                screen_ref[q, n, start : start + block, :LANES] = cosine
                screen_ref[q, n, start : start + block, LANES:] = sine
    for copy in copies:
        copy.wait()


def screens(offsets, neighbours, rotate, w_values, table_r, table_c):
    planes = w_values.shape[0]
    groups, n_columns = len(offsets), len(neighbours)
    half = table_c.shape[2]
    tables = [pltpu.with_memory_space_constraint(value, HBM) for value in (table_r, table_c)]
    return pl.pallas_call(
        functools.partial(screen_kernel, offsets, neighbours, rotate),
        in_specs=[pl.BlockSpec(memory_space=SMEM)] + [pl.BlockSpec(memory_space=HBM)] * 2,
        out_specs=[pl.BlockSpec(memory_space=VMEM)] * (3 + n_columns),
        out_shape=[
            jax.ShapeDtypeStruct((planes, groups, half, 2 * LANES), jnp.float32),
            jax.ShapeDtypeStruct((planes, groups, 1, 2 * LANES), jnp.float32),
            jax.ShapeDtypeStruct(table_r.shape[1:], jnp.bfloat16),
        ]
        + [jax.ShapeDtypeStruct(table_c.shape[1:], jnp.bfloat16)] * n_columns,
        scratch_shapes=[pltpu.SemaphoreType.DMA((1 + n_columns,))],
        compiler_params=pltpu.CompilerParams(vmem_limit_bytes=24 << 20),
        cost_estimate=pl.CostEstimate(
            flops=planes * half * NV * 20, bytes_accessed=planes * half * NV * 4, transcendentals=0
        ),
        name="screens",
    )(w_values, *tables)


def row_kernel_body(offsets, rotate, own_ref, recv_ref, table_r, *outs):
    planes, rows, _ = own_ref.shape
    groups = table_r.shape[0]
    grid = (own_ref[...] + recv_ref[...].astype(jnp.float32)).astype(jnp.bfloat16)
    grid = grid.reshape(planes * rows, NV)
    for out_ref, k in zip(outs, offsets):
        g = lax.axis_index("img") ^ k if rotate else k
        out_ref[...] = jnp.dot(grid, table_r[g], preferred_element_type=jnp.float32).astype(
            jnp.bfloat16
        )


def row_transform(offsets, rotate, own, recv, table_r):
    planes, rows, _ = own.shape
    one = jax.ShapeDtypeStruct((planes * rows, 2 * LANES), jnp.bfloat16)
    return pl.pallas_call(
        functools.partial(row_kernel_body, offsets, rotate),
        in_specs=[pl.BlockSpec(memory_space=VMEM)] * 3,
        out_specs=[pl.BlockSpec(memory_space=VMEM)] * len(offsets),
        out_shape=[one] * len(offsets),
        compiler_params=pltpu.CompilerParams(vmem_limit_bytes=24 << 20),
        name="row_dft",
    )(own, recv, table_r)


def image_kernel(count, depth, first_screen, *refs):
    rowdft = refs[: count * depth]
    tables = refs[count * depth : (count + 1) * depth]
    screen_ref, middle_ref, *outs, back = refs[(count + 1) * depth :]
    planes = screen_ref.shape[0]
    rows = rowdft[0].shape[0] // planes
    wa = lax.axis_index("wa")
    wa_count, piece = outs[0].shape[0], outs[0].shape[1]
    half = tables[0].shape[1]
    block = LANES
    row_at = lax.broadcasted_iota(jnp.int32, (half, half), 0)
    col_at = lax.broadcasted_iota(jnp.int32, (half, half), 1)
    flip = (row_at == jnp.where(col_at == 0, 0, half - col_at)).astype(jnp.bfloat16)

    def put(start, count, n, value):
        for j in range(count // piece):
            at = lax.rem(start // piece + j - wa + wa_count, wa_count)
            outs[n][at] = value[j * piece : (j + 1) * piece]

    for n in range(count):
        at_screen = first_screen + n
        firsts = []
        for start in range(0, half, block):
            even = jnp.zeros((block, LANES), jnp.float32)
            odd = jnp.zeros((block, LANES), jnp.float32)
            for q in range(planes):
                by_cos, by_sin = (
                    sum(
                        jnp.dot(
                            tables[d][which, start : start + block],
                            rowdft[n * depth + d][q * rows : (q + 1) * rows],
                            preferred_element_type=jnp.float32,
                        )
                        for d in range(depth)
                    )
                    for which in range(2)
                )
                cosine = screen_ref[q, at_screen, start : start + block, :LANES]
                sine = screen_ref[q, at_screen, start : start + block, LANES:]
                even += cosine * by_cos[:, :LANES] - sine * by_cos[:, LANES:]
                if start == 0:
                    row = lax.broadcasted_iota(jnp.int32, (block, 1), 0)
                    cosine, sine = (
                        jnp.where(row == 0, -middle_ref[q, at_screen, :, LANES:], cosine),
                        jnp.where(row == 0, middle_ref[q, at_screen, :, :LANES], sine),
                    )
                odd += cosine * by_sin[:, LANES:] + sine * by_sin[:, :LANES]
            low, high = even - odd, even + odd
            if start == 0:
                low = jnp.where(row == 0, even, low)
                high = jnp.where(row == 0, odd, high)
            firsts.append(low.astype(jnp.bfloat16))
            back[start : start + block] = high.astype(jnp.bfloat16)
        put(0, half, n, jnp.concatenate(firsts, axis=0))
        second = jnp.dot(flip, back[...], preferred_element_type=jnp.float32).astype(jnp.bfloat16)
        put(half, half, n, second)


def images(count, wa_count, first_screen, rowdft, tables, screen, middle):
    half = tables[0].shape[1]
    inputs = (*rowdft, *tables, screen, middle)
    one = jax.ShapeDtypeStruct((wa_count, 2 * half // wa_count, LANES), jnp.bfloat16)
    return pl.pallas_call(
        functools.partial(image_kernel, count, len(tables), first_screen),
        in_specs=[pl.BlockSpec(memory_space=VMEM)] * len(inputs),
        out_specs=[pl.BlockSpec(memory_space=VMEM)] * count,
        out_shape=[one] * count,
        scratch_shapes=[VMEM((half, LANES), jnp.bfloat16)],
        compiler_params=pltpu.CompilerParams(vmem_limit_bytes=24 << 20),
        name=f"image_{count}_{len(tables)}",
    )(*inputs)


def add_kernel(one_ref, *refs):
    total = one_ref[...].astype(jnp.float32)
    for ref in refs[:-1]:
        total += ref[...].astype(jnp.float32)
    refs[-1][...] = total.astype(refs[-1].dtype)


def add_rounded(*parts):
    return pl.pallas_call(
        add_kernel,
        in_specs=[pl.BlockSpec(memory_space=VMEM)] * len(parts),
        out_specs=pl.BlockSpec(memory_space=VMEM),
        out_shape=jax.ShapeDtypeStruct(parts[0].shape, jnp.bfloat16),
        compiler_params=pltpu.CompilerParams(vmem_limit_bytes=24 << 20),
        name="add",
    )(*parts)


def add_up(*parts):
    return sum(part.astype(jnp.float32) for part in parts)


def final_kernel(scale, mine_ref, other_ref, out_ref):
    blk = lax.axis_index("blk")
    count = mine_ref.shape[1]
    source = lax.broadcasted_iota(jnp.int32, (2 * count, 2 * count), 0)
    target = lax.broadcasted_iota(jnp.int32, (2 * count, 2 * count), 1)
    wanted = jnp.where(source < count, 2 * source + blk, 2 * (source - count) + 1 - blk)
    place = (wanted == target).astype(jnp.bfloat16)
    rest = jnp.concatenate([mine_ref[...], other_ref[...].astype(jnp.float32)], axis=1) * scale
    total = jnp.zeros(out_ref.shape, jnp.float32)
    for _ in range(3):
        term = rest.astype(jnp.bfloat16)
        total += jnp.dot(term, place, preferred_element_type=jnp.float32)
        rest = rest - term.astype(jnp.float32)
    out_ref[...] = total


def interleave(mine, other, scale):
    return pl.pallas_call(
        functools.partial(final_kernel, scale),
        in_specs=[pl.BlockSpec(memory_space=VMEM)] * 2,
        out_specs=pl.BlockSpec(memory_space=VMEM),
        out_shape=jax.ShapeDtypeStruct((mine.shape[0], 2 * mine.shape[1]), jnp.float32),
        compiler_params=pltpu.CompilerParams(vmem_limit_bytes=24 << 20),
        name="interleave",
    )(mine, other)


def shift(value, axis, by):
    count = lax.axis_size(axis)
    return lax.ppermute(value, axis, [(one, (one + by) % count) for one in range(count)])


def swap(value, axis, bits, members=None):
    members = range(lax.axis_size(axis)) if members is None else members
    return lax.ppermute(value, axis, [(one, one ^ bits) for one in members])


def shards(
    visibilities, row_kernel, col_kernel, block_mask, tile_counts, tile_ids, tile_planes, w_values
):
    slots = tile_counts.shape[3]
    planes = w_values.shape[0]
    rows, vis_len = row_kernel.shape[4], row_kernel.shape[5]
    width = col_kernel.shape[5]
    img_count = lax.axis_size("img")
    wa_count = lax.axis_size("wa")
    full = rows * img_count
    table_r = jnp.asarray(row_table(NV // width, width), jnp.bfloat16)
    table_c = jnp.asarray(column_table(img_count, rows), jnp.bfloat16)
    own, send = gridding(
        tile_counts.reshape(slots),
        tile_ids.reshape(slots),
        tile_planes.reshape(slots),
        visibilities.reshape(2, slots, vis_len),
        block_mask.reshape(slots, -1, vis_len),
        row_kernel.reshape(slots, rows, vis_len),
        col_kernel.reshape(slots, vis_len, width),
        planes,
    )
    recv = shift(send, "blk", 1)
    groups = NV // 2 // LANES
    rotate = groups == img_count
    offsets = [3, 2, 0] if rotate else list(range(groups))
    neighbours = [0, 1] if rotate else [0]
    screen, middle, table_r, *columns = screens(
        offsets, neighbours, rotate, w_values, table_r, table_c
    )
    rowdft = row_transform([1, 3, 2, 0] if rotate else offsets, rotate, own, recv, table_r)

    def over_wa(part):
        return [shift(part[by], "wa", by) for by in range(1, wa_count)]

    if rotate:
        beside, outer, far, here = rowdft
        from_beside = swap(beside, "img", 1)
        outer, far = images(2, wa_count, 0, [outer, far], columns[:1], screen, middle)
        outer = add_rounded(outer[0], *over_wa(outer))
        far = add_rounded(far[0], *over_wa(far))
        from_outer = swap(outer, "img", 3)
        from_far = swap(far, "img", 2)
        (here,) = images(1, wa_count, 2, [here, from_beside], columns, screen, middle)
        total = add_up(here[0], *over_wa(here), from_outer, from_far)
    else:
        parts = images(groups, wa_count, 0, rowdft, columns, screen, middle)
        part = jnp.stack(parts, axis=1)
        held = add_rounded(part[0], *over_wa(part))
        held = jnp.swapaxes(held, 0, 1).reshape(full // wa_count, img_count, -1)
        held = jnp.roll(jnp.swapaxes(held, 0, 1), -lax.axis_index("img"), axis=0)
        total = add_up(held[0], *(shift(held[by], "img", by) for by in range(1, img_count)))
    blk = lax.axis_index("blk")
    total = total.reshape(2, total.shape[0] // 2, total.shape[1])
    mine = lax.dynamic_index_in_dim(total, blk, 0, keepdims=False)
    other = lax.dynamic_index_in_dim(total, 1 - blk, 0, keepdims=False)
    other = shift(other.astype(jnp.bfloat16), "blk", 1)
    return interleave(mine, other, 1.0 / math.sqrt(full * NV * planes * wa_count))


def solution(mesh):
    in_specs = (
        P(None, ("parts", "img"), "wa", "blk", None, None),
        P(("parts", "img"), "wa", "blk", None, None, None),
        P(("parts", "img"), "wa", "blk", None, None, None),
        P(("parts", "img"), "wa", "blk", None, None, None),
        P(("parts", "img"), "wa", "blk", None),
        P(("parts", "img"), "wa", "blk", None),
        P(("parts", "img"), "wa", "blk", None),
        P(("parts", "wa")),
    )
    out_specs = P(("parts", "wa", "blk"), "img")
    return jax.shard_map(shards, mesh=mesh, in_specs=in_specs, out_specs=out_specs, check_vma=False)
```

```python
import functools
import math

import jax
import jax.numpy as jnp
import numpy as np
from jax import lax
from jax.experimental import pallas as pl
from jax.experimental.pallas import tpu as pltpu
from jax.sharding import PartitionSpec as P

NV = 1024
LANES = 128
VMEM = pltpu.VMEM
SMEM = pltpu.SMEM
HBM = pltpu.HBM


def angles(first, second, length):
    return 2.0 * np.pi / length * (np.outer(first, second) % length)


def row_table(across, tile_width):
    half_v = np.arange(NV // 2)
    out = []
    for parity in range(2):
        m_index = 2 * np.arange(NV // 2) + parity
        ang = angles(half_v, m_index, NV)
        cosine, sine = np.cos(ang), np.sin(ang)
        real = np.stack([cosine, -sine])
        imag = np.stack([sine, cosine])
        both = np.stack([real, imag])
        both = both.reshape(2, 2, across // 2, tile_width, NV // 2 // LANES, LANES)
        out.append(both.transpose(4, 2, 1, 3, 0, 5).reshape(-1, NV, 2 * LANES))
    return np.stack(out)


def column_table(img_count, rows):
    full = img_count * rows
    ang = angles(np.arange(full // 2), np.arange(full), full)
    cosine, sine = np.cos(ang), np.sin(ang)
    sine[0] = np.cos(np.pi * (np.arange(full) % 2))
    both = np.stack([cosine, sine]).reshape(2, full // 2, img_count, rows)
    return both.transpose(2, 0, 1, 3)


def grid_kernel(
    counts_hbm,
    ids_hbm,
    planes_hbm,
    vis_hbm,
    mask_hbm,
    rk_hbm,
    ck_hbm,
    own_ref,
    send_ref,
    counts_ref,
    ids_ref,
    planes_ref,
    vis_ref,
    mask_ref,
    rk_ref,
    ck_ref,
    acc,
    small_sem,
    rk_sem,
    ck_sem,
):
    blk = lax.axis_index("blk")
    slots, rows, vis_len = rk_ref.shape
    codes = acc.shape[0]
    width = ck_ref.shape[2]
    blocks = mask_ref.shape[1]
    planes = own_ref.shape[0]
    across = codes // planes
    chunks = rk_sem.shape[0]
    group = slots // chunks

    small = [
        pltpu.make_async_copy(source, target, small_sem.at[n])
        for n, (source, target) in enumerate(
            [
                (counts_hbm, counts_ref),
                (ids_hbm, ids_ref),
                (planes_hbm, planes_ref),
                (vis_hbm, vis_ref),
                (mask_hbm, mask_ref),
            ]
        )
    ]
    large = []
    for n in range(chunks):
        part = pl.ds(n * group, group)
        large.append(
            [
                pltpu.make_async_copy(ck_hbm.at[part], ck_ref.at[part], ck_sem.at[n]),
                pltpu.make_async_copy(rk_hbm.at[part], rk_ref.at[part], rk_sem.at[n]),
            ]
        )
    for copy in small + sum(large, []):
        copy.start()
    acc[...] = jnp.zeros_like(acc)
    for copy in small:
        copy.wait()

    lane = lax.broadcasted_iota(jnp.int32, (1, vis_len), 1)
    real, imag = [], []
    for slot in range(slots):
        mask = mask_ref[slot].astype(jnp.float32) * (lane < counts_ref[slot]).astype(jnp.float32)
        real.append(mask * vis_ref[0, pl.ds(slot, 1), :].astype(jnp.float32))
        imag.append(mask * vis_ref[1, pl.ds(slot, 1), :].astype(jnp.float32))
    scaled = [jnp.concatenate(value, axis=0).T for value in (real, imag)]
    block_of = lax.broadcasted_iota(jnp.int32, (vis_len, width), 1) // (width // blocks)
    per = width // blocks
    for slot in range(slots):
        if slot % group == 0:
            for copy in large[slot // group]:
                copy.wait()
        here = slice(slot // per * width, (slot // per + 1) * width)
        source = block_of + slot % per * blocks
        weighted = jnp.concatenate(
            [
                jnp.take_along_axis(value[:, here], source, axis=1).astype(jnp.bfloat16)
                * ck_ref[slot]
                for value in scaled
            ],
            axis=1,
        )
        tile = jnp.dot(rk_ref[slot], weighted, preferred_element_type=jnp.float32)
        acc[planes_ref[slot] * across + ids_ref[slot]] += tile

    sign = (1 - 2 * blk).astype(jnp.float32)
    for plane in range(planes):
        for t in range(across // 2):
            low = acc[plane * across + t]
            high = acc[plane * across + t + across // 2] * sign
            where = pl.ds(t * 2 * width, 2 * width)
            own_ref[plane, :, where] = (low + high).astype(jnp.bfloat16)
            send_ref[plane, :, where] = (low - high).astype(jnp.bfloat16)


def gridding(counts, ids, levels, vis, mask, rk, ck, planes):
    slots, rows, vis_len = rk.shape
    width = ck.shape[2]
    across = NV // width
    chunks = 2
    half = (planes, rows, NV)
    inputs = (counts, ids, levels, vis, mask, rk, ck)
    return pl.pallas_call(
        grid_kernel,
        in_specs=[pl.BlockSpec(memory_space=HBM)] * len(inputs),
        out_specs=[pl.BlockSpec(memory_space=VMEM)] * 2,
        out_shape=[jax.ShapeDtypeStruct(half, jnp.bfloat16)] * 2,
        scratch_shapes=[SMEM(counts.shape, jnp.int32)] * 3
        + [VMEM(value.shape, value.dtype) for value in (vis, mask, rk, ck)]
        + [
            VMEM((planes * across, rows, 2 * width), jnp.float32),
            pltpu.SemaphoreType.DMA((5,)),
            pltpu.SemaphoreType.DMA((chunks,)),
            pltpu.SemaphoreType.DMA((chunks,)),
        ],
        compiler_params=pltpu.CompilerParams(vmem_limit_bytes=24 << 20),
        name="gridding",
    )(*(pltpu.with_memory_space_constraint(value, HBM) for value in inputs))


COS_POLY = np.polynomial.chebyshev.Chebyshev.interpolate(
    lambda z: np.cos(2 * np.pi * np.sqrt(np.maximum(z, 0.0))), 5, [0.0, 0.25]
).convert(kind=np.polynomial.Polynomial).coef
SIN_POLY = np.polynomial.chebyshev.Chebyshev.interpolate(
    lambda z: np.sinc(2 * np.sqrt(np.maximum(z, 0.0))) * 2 * np.pi, 5, [0.0, 0.25]
).convert(kind=np.polynomial.Polynomial).coef


def horner(coef, z):
    total = jnp.full_like(z, float(coef[-1]))
    for value in coef[-2::-1]:
        total = total * z + float(value)
    return total


def turn(cycles):
    rest = cycles - jnp.round(cycles)
    square = rest * rest
    return horner(COS_POLY, square), horner(SIN_POLY, square) * rest


def screen_kernel(
    offsets, neighbours, rotate, w_ref, table_r_hbm, table_c_hbm, screen_ref, middle_ref, table_r_ref, *refs
):
    columns, sem = refs[:-1], refs[-1]
    img = lax.axis_index("img")
    copies = [pltpu.make_async_copy(table_r_hbm.at[lax.axis_index("blk")], table_r_ref, sem.at[0])]
    for n, ref in enumerate(columns):
        source = table_c_hbm.at[img ^ neighbours[n]]
        copies.append(pltpu.make_async_copy(source, ref, sem.at[1 + n]))
    for copy in copies:
        copy.start()
    planes, _, half, _ = screen_ref.shape
    full = 2 * half
    blk = lax.axis_index("blk")
    block = LANES
    for n, k in enumerate(offsets):
        g = lax.axis_index("img") ^ k if rotate else k
        column = 2 * (g * LANES + lax.broadcasted_iota(jnp.int32, (1, LANES), 1)) + blk
        y = (column.astype(jnp.float32) - NV / 2) / NV
        rest_y = 1.0 - y * y
        for q in range(planes):
            cosine, sine = turn((jnp.sqrt(rest_y) - 1.0) * w_ref[q])
            middle_ref[q, n] = jnp.concatenate([cosine, sine], axis=1)
        for start in range(0, half, block):
            row = start + lax.broadcasted_iota(jnp.int32, (block, 1), 0)
            x = (row.astype(jnp.float32) - half) / full
            nterm = jnp.sqrt(rest_y - x * x) - 1.0
            for q in range(planes):
                cosine, sine = turn(nterm * w_ref[q])
                screen_ref[q, n, start : start + block, :LANES] = cosine
                screen_ref[q, n, start : start + block, LANES:] = sine
    for copy in copies:
        copy.wait()


def screens(offsets, neighbours, rotate, w_values, table_r, table_c):
    planes = w_values.shape[0]
    groups, n_columns = len(offsets), len(neighbours)
    half = table_c.shape[2]
    tables = [pltpu.with_memory_space_constraint(value, HBM) for value in (table_r, table_c)]
    return pl.pallas_call(
        functools.partial(screen_kernel, offsets, neighbours, rotate),
        in_specs=[pl.BlockSpec(memory_space=SMEM)] + [pl.BlockSpec(memory_space=HBM)] * 2,
        out_specs=[pl.BlockSpec(memory_space=VMEM)] * (3 + n_columns),
        out_shape=[
            jax.ShapeDtypeStruct((planes, groups, half, 2 * LANES), jnp.float32),
            jax.ShapeDtypeStruct((planes, groups, 1, 2 * LANES), jnp.float32),
            jax.ShapeDtypeStruct(table_r.shape[1:], jnp.bfloat16),
        ]
        + [jax.ShapeDtypeStruct(table_c.shape[1:], jnp.bfloat16)] * n_columns,
        scratch_shapes=[pltpu.SemaphoreType.DMA((1 + n_columns,))],
        compiler_params=pltpu.CompilerParams(vmem_limit_bytes=24 << 20),
        cost_estimate=pl.CostEstimate(
            flops=planes * half * NV * 20, bytes_accessed=planes * half * NV * 4, transcendentals=0
        ),
        name="screens",
    )(w_values, *tables)


def row_kernel_body(offsets, rotate, own_ref, recv_ref, table_r, *outs):
    planes, rows, _ = own_ref.shape
    groups = table_r.shape[0]
    grid = (own_ref[...] + recv_ref[...]).reshape(planes * rows, NV)
    for out_ref, k in zip(outs, offsets):
        g = lax.axis_index("img") ^ k if rotate else k
        out_ref[...] = jnp.dot(grid, table_r[g], preferred_element_type=jnp.float32).astype(
            jnp.bfloat16
        )


def row_transform(offsets, rotate, own, recv, table_r):
    planes, rows, _ = own.shape
    one = jax.ShapeDtypeStruct((planes * rows, 2 * LANES), jnp.bfloat16)
    return pl.pallas_call(
        functools.partial(row_kernel_body, offsets, rotate),
        in_specs=[pl.BlockSpec(memory_space=VMEM)] * 3,
        out_specs=[pl.BlockSpec(memory_space=VMEM)] * len(offsets),
        out_shape=[one] * len(offsets),
        compiler_params=pltpu.CompilerParams(vmem_limit_bytes=24 << 20),
        name="row_dft",
    )(own, recv, table_r)


def image_kernel(count, depth, first_screen, *refs):
    rowdft = refs[: count * depth]
    tables = refs[count * depth : (count + 1) * depth]
    screen_ref, middle_ref, *outs, back = refs[(count + 1) * depth :]
    planes = screen_ref.shape[0]
    rows = rowdft[0].shape[0] // planes
    wa = lax.axis_index("wa")
    wa_count, piece = outs[0].shape[0], outs[0].shape[1]
    half = tables[0].shape[1]
    block = LANES
    row_at = lax.broadcasted_iota(jnp.int32, (half, half), 0)
    col_at = lax.broadcasted_iota(jnp.int32, (half, half), 1)
    flip = (row_at == jnp.where(col_at == 0, 0, half - col_at)).astype(jnp.bfloat16)

    def put(start, count, n, value):
        for j in range(count // piece):
            at = lax.rem(start // piece + j - wa + wa_count, wa_count)
            outs[n][at] = value[j * piece : (j + 1) * piece]

    for n in range(count):
        at_screen = first_screen + n
        firsts = []
        for start in range(0, half, block):
            even = jnp.zeros((block, LANES), jnp.float32)
            odd = jnp.zeros((block, LANES), jnp.float32)
            for q in range(planes):
                by_cos, by_sin = (
                    sum(
                        jnp.dot(
                            tables[d][which, start : start + block],
                            rowdft[n * depth + d][q * rows : (q + 1) * rows],
                            preferred_element_type=jnp.float32,
                        )
                        for d in range(depth)
                    )
                    for which in range(2)
                )
                cosine = screen_ref[q, at_screen, start : start + block, :LANES]
                sine = screen_ref[q, at_screen, start : start + block, LANES:]
                even += cosine * by_cos[:, :LANES] - sine * by_cos[:, LANES:]
                if start == 0:
                    row = lax.broadcasted_iota(jnp.int32, (block, 1), 0)
                    cosine, sine = (
                        jnp.where(row == 0, -middle_ref[q, at_screen, :, LANES:], cosine),
                        jnp.where(row == 0, middle_ref[q, at_screen, :, :LANES], sine),
                    )
                odd += cosine * by_sin[:, LANES:] + sine * by_sin[:, :LANES]
            low, high = even - odd, even + odd
            if start == 0:
                low = jnp.where(row == 0, even, low)
                high = jnp.where(row == 0, odd, high)
            firsts.append(low.astype(jnp.bfloat16))
            back[start : start + block] = high.astype(jnp.bfloat16)
        put(0, half, n, jnp.concatenate(firsts, axis=0))
        second = jnp.dot(flip, back[...], preferred_element_type=jnp.float32).astype(jnp.bfloat16)
        put(half, half, n, second)


def first_kernel(offsets, own_ref, recv_ref, table_r, table_c, screen_ref, middle_ref, *refs):
    *outs, rowdft, back = refs
    count = rowdft.shape[0]
    blocks = [rowdft.at[n] for n in range(count)]
    row_kernel_body(offsets, True, own_ref, recv_ref, table_r, *blocks, *outs[count:])
    image_kernel(count, 1, 0, *blocks, table_c, screen_ref, middle_ref, *outs[:count], back)


def first_images(offsets, count, wa_count, own, recv, table_r, table_c, screen, middle):
    half = table_c.shape[1]
    planes, rows, _ = own.shape
    inputs = (own, recv, table_r, table_c, screen, middle)
    image = jax.ShapeDtypeStruct((wa_count, 2 * half // wa_count, LANES), jnp.bfloat16)
    block = jax.ShapeDtypeStruct((planes * rows, 2 * LANES), jnp.bfloat16)
    return pl.pallas_call(
        functools.partial(first_kernel, offsets),
        in_specs=[pl.BlockSpec(memory_space=VMEM)] * len(inputs),
        out_specs=[pl.BlockSpec(memory_space=VMEM)] * len(offsets),
        out_shape=[image] * count + [block] * (len(offsets) - count),
        scratch_shapes=[
            VMEM((count, planes * rows, 2 * LANES), jnp.bfloat16),
            VMEM((half, LANES), jnp.bfloat16),
        ],
        compiler_params=pltpu.CompilerParams(vmem_limit_bytes=24 << 20),
        name="first_images",
    )(*inputs)


def images(count, wa_count, first_screen, rowdft, tables, screen, middle):
    half = tables[0].shape[1]
    inputs = (*rowdft, *tables, screen, middle)
    one = jax.ShapeDtypeStruct((wa_count, 2 * half // wa_count, LANES), jnp.bfloat16)
    return pl.pallas_call(
        functools.partial(image_kernel, count, len(tables), first_screen),
        in_specs=[pl.BlockSpec(memory_space=VMEM)] * len(inputs),
        out_specs=[pl.BlockSpec(memory_space=VMEM)] * count,
        out_shape=[one] * count,
        scratch_shapes=[VMEM((half, LANES), jnp.bfloat16)],
        compiler_params=pltpu.CompilerParams(vmem_limit_bytes=24 << 20),
        name=f"image_{count}_{len(tables)}",
    )(*inputs)


def add_kernel(one_ref, *refs):
    total = one_ref[...].astype(jnp.float32)
    for ref in refs[:-1]:
        total += ref[...].astype(jnp.float32)
    refs[-1][...] = total.astype(refs[-1].dtype)


def add_rounded(*parts):
    return pl.pallas_call(
        add_kernel,
        in_specs=[pl.BlockSpec(memory_space=VMEM)] * len(parts),
        out_specs=pl.BlockSpec(memory_space=VMEM),
        out_shape=jax.ShapeDtypeStruct(parts[0].shape, jnp.bfloat16),
        compiler_params=pltpu.CompilerParams(vmem_limit_bytes=24 << 20),
        name="add",
    )(*parts)


def add_up(*parts):
    return sum(part.astype(jnp.float32) for part in parts)


def final_kernel(scale, mine_ref, other_ref, out_ref):
    blk = lax.axis_index("blk")
    count = mine_ref.shape[1]
    source = lax.broadcasted_iota(jnp.int32, (2 * count, 2 * count), 0)
    target = lax.broadcasted_iota(jnp.int32, (2 * count, 2 * count), 1)
    wanted = jnp.where(source < count, 2 * source + blk, 2 * (source - count) + 1 - blk)
    place = (wanted == target).astype(jnp.bfloat16)
    rest = jnp.concatenate([mine_ref[...], other_ref[...].astype(jnp.float32)], axis=1) * scale
    total = jnp.zeros(out_ref.shape, jnp.float32)
    for _ in range(3):
        term = rest.astype(jnp.bfloat16)
        total += jnp.dot(term, place, preferred_element_type=jnp.float32)
        rest = rest - term.astype(jnp.float32)
    out_ref[...] = total


def interleave(mine, other, scale):
    return pl.pallas_call(
        functools.partial(final_kernel, scale),
        in_specs=[pl.BlockSpec(memory_space=VMEM)] * 2,
        out_specs=pl.BlockSpec(memory_space=VMEM),
        out_shape=jax.ShapeDtypeStruct((mine.shape[0], 2 * mine.shape[1]), jnp.float32),
        compiler_params=pltpu.CompilerParams(vmem_limit_bytes=24 << 20),
        name="interleave",
    )(mine, other)


def shift(value, axis, by):
    count = lax.axis_size(axis)
    return lax.ppermute(value, axis, [(one, (one + by) % count) for one in range(count)])


def swap(value, axis, bits, members=None):
    members = range(lax.axis_size(axis)) if members is None else members
    return lax.ppermute(value, axis, [(one, one ^ bits) for one in members])


def shards(
    visibilities, row_kernel, col_kernel, block_mask, tile_counts, tile_ids, tile_planes, w_values
):
    slots = tile_counts.shape[3]
    planes = w_values.shape[0]
    rows, vis_len = row_kernel.shape[4], row_kernel.shape[5]
    width = col_kernel.shape[5]
    img_count = lax.axis_size("img")
    wa_count = lax.axis_size("wa")
    full = rows * img_count
    table_r = jnp.asarray(row_table(NV // width, width), jnp.bfloat16)
    table_c = jnp.asarray(column_table(img_count, rows), jnp.bfloat16)
    own, send = gridding(
        tile_counts.reshape(slots),
        tile_ids.reshape(slots),
        tile_planes.reshape(slots),
        visibilities.reshape(2, slots, vis_len),
        block_mask.reshape(slots, -1, vis_len),
        row_kernel.reshape(slots, rows, vis_len),
        col_kernel.reshape(slots, vis_len, width),
        planes,
    )
    recv = shift(send, "blk", 1)
    groups = NV // 2 // LANES
    rotate = groups == img_count
    offsets = [3, 2, 0] if rotate else list(range(groups))
    neighbours = [0, 1] if rotate else [0]
    screen, middle, table_r, *columns = screens(
        offsets, neighbours, rotate, w_values, table_r, table_c
    )

    def over_wa(part):
        return [shift(part[by], "wa", by) for by in range(1, wa_count)]

    if rotate:
        outer, far, beside, here = first_images(
            [3, 2, 1, 0], 2, wa_count, own, recv, table_r, columns[0], screen, middle
        )
        from_beside = swap(beside, "img", 1)
        outer = add_rounded(outer[0], *over_wa(outer))
        far = add_rounded(far[0], *over_wa(far))
        from_outer = swap(outer, "img", 3)
        from_far = swap(far, "img", 2)
        (here,) = images(1, wa_count, 2, [here, from_beside], columns, screen, middle)
        total = add_up(here[0], *over_wa(here), from_outer, from_far)
    else:
        rowdft = row_transform(offsets, rotate, own, recv, table_r)
        parts = images(groups, wa_count, 0, rowdft, columns, screen, middle)
        part = jnp.stack(parts, axis=1)
        held = add_rounded(part[0], *over_wa(part))
        held = jnp.swapaxes(held, 0, 1).reshape(full // wa_count, img_count, -1)
        held = jnp.roll(jnp.swapaxes(held, 0, 1), -lax.axis_index("img"), axis=0)
        total = add_up(held[0], *(shift(held[by], "img", by) for by in range(1, img_count)))
    blk = lax.axis_index("blk")
    total = total.reshape(2, total.shape[0] // 2, total.shape[1])
    mine = lax.dynamic_index_in_dim(total, blk, 0, keepdims=False)
    other = lax.dynamic_index_in_dim(total, 1 - blk, 0, keepdims=False)
    other = shift(other.astype(jnp.bfloat16), "blk", 1)
    return interleave(mine, other, 1.0 / math.sqrt(full * NV * planes * wa_count))


def solution(mesh):
    in_specs = (
        P(None, ("parts", "img"), "wa", "blk", None, None),
        P(("parts", "img"), "wa", "blk", None, None, None),
        P(("parts", "img"), "wa", "blk", None, None, None),
        P(("parts", "img"), "wa", "blk", None, None, None),
        P(("parts", "img"), "wa", "blk", None),
        P(("parts", "img"), "wa", "blk", None),
        P(("parts", "img"), "wa", "blk", None),
        P(("parts", "wa")),
    )
    out_specs = P(("parts", "wa", "blk"), "img")
    return jax.shard_map(shards, mesh=mesh, in_specs=in_specs, out_specs=out_specs, check_vma=False)
```

```python
import functools
import math

import jax
import jax.numpy as jnp
import numpy as np
from jax import lax
from jax.experimental import pallas as pl
from jax.experimental.pallas import tpu as pltpu
from jax.sharding import PartitionSpec as P

NV = 1024
LANES = 128
VMEM = pltpu.VMEM
SMEM = pltpu.SMEM
HBM = pltpu.HBM


def angles(first, second, length):
    return 2.0 * np.pi / length * (np.outer(first, second) % length)


def row_table(across, tile_width):
    half_v = np.arange(NV // 2)
    out = []
    for parity in range(2):
        m_index = 2 * np.arange(NV // 2) + parity
        ang = angles(half_v, m_index, NV)
        cosine, sine = np.cos(ang), np.sin(ang)
        real = np.stack([cosine, -sine])
        imag = np.stack([sine, cosine])
        both = np.stack([real, imag])
        both = both.reshape(2, 2, across // 2, tile_width, NV // 2 // LANES, LANES)
        out.append(both.transpose(4, 2, 1, 3, 0, 5).reshape(-1, NV, 2 * LANES))
    return np.stack(out)


def column_table(img_count, rows):
    full = img_count * rows
    ang = angles(np.arange(full // 2), np.arange(full), full)
    cosine, sine = np.cos(ang), np.sin(ang)
    sine[0] = np.cos(np.pi * (np.arange(full) % 2))
    both = np.stack([cosine, sine]).reshape(2, full // 2, img_count, rows)
    return both.transpose(2, 0, 1, 3)


def grid_kernel(
    counts_hbm,
    ids_hbm,
    planes_hbm,
    vis_hbm,
    mask_hbm,
    rk_hbm,
    ck_hbm,
    own_ref,
    send_ref,
    counts_ref,
    ids_ref,
    planes_ref,
    vis_ref,
    mask_ref,
    rk_ref,
    ck_ref,
    acc,
    small_sem,
    rk_sem,
    ck_sem,
):
    blk = lax.axis_index("blk")
    slots, rows, vis_len = rk_ref.shape
    codes = acc.shape[0]
    width = ck_ref.shape[2]
    blocks = mask_ref.shape[1]
    planes = own_ref.shape[0]
    across = codes // planes
    chunks = rk_sem.shape[0]
    group = slots // chunks

    small = [
        pltpu.make_async_copy(source, target, small_sem.at[n])
        for n, (source, target) in enumerate(
            [
                (counts_hbm, counts_ref),
                (ids_hbm, ids_ref),
                (planes_hbm, planes_ref),
                (vis_hbm, vis_ref),
                (mask_hbm, mask_ref),
            ]
        )
    ]
    large = []
    for n in range(chunks):
        part = pl.ds(n * group, group)
        large.append(
            [
                pltpu.make_async_copy(ck_hbm.at[part], ck_ref.at[part], ck_sem.at[n]),
                pltpu.make_async_copy(rk_hbm.at[part], rk_ref.at[part], rk_sem.at[n]),
            ]
        )
    for copy in small + sum(large, []):
        copy.start()
    acc[...] = jnp.zeros_like(acc)
    for copy in small:
        copy.wait()

    lane = lax.broadcasted_iota(jnp.int32, (1, vis_len), 1)
    real, imag = [], []
    for slot in range(slots):
        mask = mask_ref[slot].astype(jnp.float32) * (lane < counts_ref[slot]).astype(jnp.float32)
        real.append(mask * vis_ref[0, pl.ds(slot, 1), :].astype(jnp.float32))
        imag.append(mask * vis_ref[1, pl.ds(slot, 1), :].astype(jnp.float32))
    scaled = [jnp.concatenate(value, axis=0).T for value in (real, imag)]
    block_of = lax.broadcasted_iota(jnp.int32, (vis_len, width), 1) // (width // blocks)
    per = width // blocks
    for slot in range(slots):
        if slot % group == 0:
            for copy in large[slot // group]:
                copy.wait()
        here = slice(slot // per * width, (slot // per + 1) * width)
        source = block_of + slot % per * blocks
        weighted = jnp.concatenate(
            [
                jnp.take_along_axis(value[:, here], source, axis=1).astype(jnp.bfloat16)
                * ck_ref[slot]
                for value in scaled
            ],
            axis=1,
        )
        tile = jnp.dot(rk_ref[slot], weighted, preferred_element_type=jnp.float32)
        acc[planes_ref[slot] * across + ids_ref[slot]] += tile

    sign = (1 - 2 * blk).astype(jnp.float32)
    for plane in range(planes):
        for t in range(across // 2):
            low = acc[plane * across + t]
            high = acc[plane * across + t + across // 2] * sign
            where = pl.ds(t * 2 * width, 2 * width)
            own_ref[plane, :, where] = (low + high).astype(jnp.bfloat16)
            send_ref[plane, :, where] = (low - high).astype(jnp.bfloat16)


def gridding(counts, ids, levels, vis, mask, rk, ck, planes):
    slots, rows, vis_len = rk.shape
    width = ck.shape[2]
    across = NV // width
    chunks = 2
    half = (planes, rows, NV)
    inputs = (counts, ids, levels, vis, mask, rk, ck)
    return pl.pallas_call(
        grid_kernel,
        in_specs=[pl.BlockSpec(memory_space=HBM)] * len(inputs),
        out_specs=[pl.BlockSpec(memory_space=VMEM)] * 2,
        out_shape=[jax.ShapeDtypeStruct(half, jnp.bfloat16)] * 2,
        scratch_shapes=[SMEM(counts.shape, jnp.int32)] * 3
        + [VMEM(value.shape, value.dtype) for value in (vis, mask, rk, ck)]
        + [
            VMEM((planes * across, rows, 2 * width), jnp.float32),
            pltpu.SemaphoreType.DMA((5,)),
            pltpu.SemaphoreType.DMA((chunks,)),
            pltpu.SemaphoreType.DMA((chunks,)),
        ],
        compiler_params=pltpu.CompilerParams(vmem_limit_bytes=24 << 20),
        name="gridding",
    )(*(pltpu.with_memory_space_constraint(value, HBM) for value in inputs))


COS_POLY = np.polynomial.chebyshev.Chebyshev.interpolate(
    lambda z: np.cos(2 * np.pi * np.sqrt(np.maximum(z, 0.0))), 5, [0.0, 0.25]
).convert(kind=np.polynomial.Polynomial).coef
SIN_POLY = np.polynomial.chebyshev.Chebyshev.interpolate(
    lambda z: np.sinc(2 * np.sqrt(np.maximum(z, 0.0))) * 2 * np.pi, 5, [0.0, 0.25]
).convert(kind=np.polynomial.Polynomial).coef


def horner(coef, z):
    total = jnp.full_like(z, float(coef[-1]))
    for value in coef[-2::-1]:
        total = total * z + float(value)
    return total


def turn(cycles):
    rest = cycles - jnp.round(cycles)
    square = rest * rest
    return horner(COS_POLY, square), horner(SIN_POLY, square) * rest


def screen_kernel(
    offsets, neighbours, rotate, w_ref, table_r_hbm, table_c_hbm, screen_ref, middle_ref, table_r_ref, *refs
):
    columns, sem = refs[:-1], refs[-1]
    img = lax.axis_index("img")
    copies = [pltpu.make_async_copy(table_r_hbm.at[lax.axis_index("blk")], table_r_ref, sem.at[0])]
    for n, ref in enumerate(columns):
        source = table_c_hbm.at[img ^ neighbours[n]]
        copies.append(pltpu.make_async_copy(source, ref, sem.at[1 + n]))
    for copy in copies:
        copy.start()
    planes, _, half, _ = screen_ref.shape
    full = 2 * half
    blk = lax.axis_index("blk")
    block = LANES
    for n, k in enumerate(offsets):
        g = lax.axis_index("img") ^ k if rotate else k
        column = 2 * (g * LANES + lax.broadcasted_iota(jnp.int32, (1, LANES), 1)) + blk
        y = (column.astype(jnp.float32) - NV / 2) / NV
        rest_y = 1.0 - y * y
        for q in range(planes):
            cosine, sine = turn((jnp.sqrt(rest_y) - 1.0) * w_ref[q])
            middle_ref[q, n] = jnp.concatenate([cosine, sine], axis=1)
        for start in range(0, half, block):
            row = start + lax.broadcasted_iota(jnp.int32, (block, 1), 0)
            x = (row.astype(jnp.float32) - half) / full
            nterm = jnp.sqrt(rest_y - x * x) - 1.0
            for q in range(planes):
                cosine, sine = turn(nterm * w_ref[q])
                screen_ref[q, n, start : start + block, :LANES] = cosine
                screen_ref[q, n, start : start + block, LANES:] = sine
    for copy in copies:
        copy.wait()


def screens(offsets, neighbours, rotate, w_values, table_r, table_c):
    planes = w_values.shape[0]
    groups, n_columns = len(offsets), len(neighbours)
    half = table_c.shape[2]
    tables = [pltpu.with_memory_space_constraint(value, HBM) for value in (table_r, table_c)]
    return pl.pallas_call(
        functools.partial(screen_kernel, offsets, neighbours, rotate),
        in_specs=[pl.BlockSpec(memory_space=SMEM)] + [pl.BlockSpec(memory_space=HBM)] * 2,
        out_specs=[pl.BlockSpec(memory_space=VMEM)] * (3 + n_columns),
        out_shape=[
            jax.ShapeDtypeStruct((planes, groups, half, 2 * LANES), jnp.float32),
            jax.ShapeDtypeStruct((planes, groups, 1, 2 * LANES), jnp.float32),
            jax.ShapeDtypeStruct(table_r.shape[1:], jnp.bfloat16),
        ]
        + [jax.ShapeDtypeStruct(table_c.shape[1:], jnp.bfloat16)] * n_columns,
        scratch_shapes=[pltpu.SemaphoreType.DMA((1 + n_columns,))],
        compiler_params=pltpu.CompilerParams(vmem_limit_bytes=24 << 20),
        cost_estimate=pl.CostEstimate(
            flops=planes * half * NV * 20, bytes_accessed=planes * half * NV * 4, transcendentals=0
        ),
        name="screens",
    )(w_values, *tables)


def row_kernel_body(offsets, rotate, own_ref, recv_ref, table_r, *outs):
    planes, rows, _ = own_ref.shape
    groups = table_r.shape[0]
    grid = (own_ref[...] + recv_ref[...]).reshape(planes * rows, NV)
    for out_ref, k in zip(outs, offsets):
        g = lax.axis_index("img") ^ k if rotate else k
        out_ref[...] = jnp.dot(grid, table_r[g], preferred_element_type=jnp.float32).astype(
            jnp.bfloat16
        )


def row_transform(offsets, rotate, own, recv, table_r):
    planes, rows, _ = own.shape
    one = jax.ShapeDtypeStruct((planes * rows, 2 * LANES), jnp.bfloat16)
    return pl.pallas_call(
        functools.partial(row_kernel_body, offsets, rotate),
        in_specs=[pl.BlockSpec(memory_space=VMEM)] * 3,
        out_specs=[pl.BlockSpec(memory_space=VMEM)] * len(offsets),
        out_shape=[one] * len(offsets),
        compiler_params=pltpu.CompilerParams(vmem_limit_bytes=24 << 20),
        name="row_dft",
    )(own, recv, table_r)


def image_kernel(count, depth, first_screen, *refs):
    rowdft = refs[: count * depth]
    tables = refs[count * depth : (count + 1) * depth]
    screen_ref, middle_ref, *outs, back = refs[(count + 1) * depth :]
    planes = screen_ref.shape[0]
    rows = rowdft[0].shape[0] // planes
    wa = lax.axis_index("wa")
    wa_count, piece = outs[0].shape[0], outs[0].shape[1]
    half = tables[0].shape[1]
    block = LANES
    row_at = lax.broadcasted_iota(jnp.int32, (block, block), 0)
    col_at = lax.broadcasted_iota(jnp.int32, (block, block), 1)
    flip = (row_at + col_at == block).astype(jnp.bfloat16)
    top = lax.broadcasted_iota(jnp.int32, (block, 1), 0) == 0

    def put(start, count, n, value):
        for j in range(count // piece):
            at = lax.rem(start // piece + j - wa + wa_count, wa_count)
            outs[n][at] = value[j * piece : (j + 1) * piece]

    for n in range(count):
        at_screen = first_screen + n
        firsts = []
        for start in range(0, half, block):
            even = jnp.zeros((block, LANES), jnp.float32)
            odd = jnp.zeros((block, LANES), jnp.float32)
            for q in range(planes):
                by_cos, by_sin = (
                    sum(
                        jnp.dot(
                            tables[d][which, start : start + block],
                            rowdft[n * depth + d][q * rows : (q + 1) * rows],
                            preferred_element_type=jnp.float32,
                        )
                        for d in range(depth)
                    )
                    for which in range(2)
                )
                cosine = screen_ref[q, at_screen, start : start + block, :LANES]
                sine = screen_ref[q, at_screen, start : start + block, LANES:]
                even += cosine * by_cos[:, :LANES] - sine * by_cos[:, LANES:]
                if start == 0:
                    row = lax.broadcasted_iota(jnp.int32, (block, 1), 0)
                    cosine, sine = (
                        jnp.where(row == 0, -middle_ref[q, at_screen, :, LANES:], cosine),
                        jnp.where(row == 0, middle_ref[q, at_screen, :, :LANES], sine),
                    )
                odd += cosine * by_sin[:, LANES:] + sine * by_sin[:, :LANES]
            low, high = even - odd, even + odd
            if start == 0:
                low = jnp.where(row == 0, even, low)
                high = jnp.where(row == 0, odd, high)
            firsts.append(low.astype(jnp.bfloat16))
            back[start : start + block] = high.astype(jnp.bfloat16)
        put(0, half, n, jnp.concatenate(firsts, axis=0))
        seconds = []
        for start in range(0, half, block):
            mirror = half - block - start
            first = back[pl.ds((half - start) % half, 16), :][:1].astype(jnp.float32)
            rest = jnp.dot(flip, back[mirror : mirror + block], preferred_element_type=jnp.float32)
            seconds.append(jnp.where(top, first, rest).astype(jnp.bfloat16))
        put(half, half, n, jnp.concatenate(seconds, axis=0))


def first_kernel(offsets, own_ref, recv_ref, table_r, table_c, screen_ref, middle_ref, *refs):
    *outs, rowdft, back = refs
    count = rowdft.shape[0]
    blocks = [rowdft.at[n] for n in range(count)]
    row_kernel_body(offsets, True, own_ref, recv_ref, table_r, *blocks, *outs[count:])
    image_kernel(count, 1, 0, *blocks, table_c, screen_ref, middle_ref, *outs[:count], back)


def first_images(offsets, count, wa_count, own, recv, table_r, table_c, screen, middle):
    half = table_c.shape[1]
    planes, rows, _ = own.shape
    inputs = (own, recv, table_r, table_c, screen, middle)
    image = jax.ShapeDtypeStruct((wa_count, 2 * half // wa_count, LANES), jnp.bfloat16)
    block = jax.ShapeDtypeStruct((planes * rows, 2 * LANES), jnp.bfloat16)
    return pl.pallas_call(
        functools.partial(first_kernel, offsets),
        in_specs=[pl.BlockSpec(memory_space=VMEM)] * len(inputs),
        out_specs=[pl.BlockSpec(memory_space=VMEM)] * len(offsets),
        out_shape=[image] * count + [block] * (len(offsets) - count),
        scratch_shapes=[
            VMEM((count, planes * rows, 2 * LANES), jnp.bfloat16),
            VMEM((half, LANES), jnp.bfloat16),
        ],
        compiler_params=pltpu.CompilerParams(vmem_limit_bytes=24 << 20),
        name="first_images",
    )(*inputs)


def images(count, wa_count, first_screen, rowdft, tables, screen, middle):
    half = tables[0].shape[1]
    inputs = (*rowdft, *tables, screen, middle)
    one = jax.ShapeDtypeStruct((wa_count, 2 * half // wa_count, LANES), jnp.bfloat16)
    return pl.pallas_call(
        functools.partial(image_kernel, count, len(tables), first_screen),
        in_specs=[pl.BlockSpec(memory_space=VMEM)] * len(inputs),
        out_specs=[pl.BlockSpec(memory_space=VMEM)] * count,
        out_shape=[one] * count,
        scratch_shapes=[VMEM((half, LANES), jnp.bfloat16)],
        compiler_params=pltpu.CompilerParams(vmem_limit_bytes=24 << 20),
        name=f"image_{count}_{len(tables)}",
    )(*inputs)


def add_kernel(one_ref, *refs):
    total = one_ref[...].astype(jnp.float32)
    for ref in refs[:-1]:
        total += ref[...].astype(jnp.float32)
    refs[-1][...] = total.astype(refs[-1].dtype)


def add_rounded(*parts):
    return pl.pallas_call(
        add_kernel,
        in_specs=[pl.BlockSpec(memory_space=VMEM)] * len(parts),
        out_specs=pl.BlockSpec(memory_space=VMEM),
        out_shape=jax.ShapeDtypeStruct(parts[0].shape, jnp.bfloat16),
        compiler_params=pltpu.CompilerParams(vmem_limit_bytes=24 << 20),
        name="add",
    )(*parts)


def add_up(*parts):
    return sum(part.astype(jnp.float32) for part in parts)


def final_kernel(scale, mine_ref, other_ref, out_ref):
    blk = lax.axis_index("blk")
    count = mine_ref.shape[1]
    source = lax.broadcasted_iota(jnp.int32, (2 * count, 2 * count), 0)
    target = lax.broadcasted_iota(jnp.int32, (2 * count, 2 * count), 1)
    wanted = jnp.where(source < count, 2 * source + blk, 2 * (source - count) + 1 - blk)
    place = (wanted == target).astype(jnp.bfloat16)
    rest = jnp.concatenate([mine_ref[...], other_ref[...].astype(jnp.float32)], axis=1) * scale
    total = jnp.zeros(out_ref.shape, jnp.float32)
    for _ in range(3):
        term = rest.astype(jnp.bfloat16)
        total += jnp.dot(term, place, preferred_element_type=jnp.float32)
        rest = rest - term.astype(jnp.float32)
    out_ref[...] = total


def interleave(mine, other, scale):
    return pl.pallas_call(
        functools.partial(final_kernel, scale),
        in_specs=[pl.BlockSpec(memory_space=VMEM)] * 2,
        out_specs=pl.BlockSpec(memory_space=VMEM),
        out_shape=jax.ShapeDtypeStruct((mine.shape[0], 2 * mine.shape[1]), jnp.float32),
        compiler_params=pltpu.CompilerParams(vmem_limit_bytes=24 << 20),
        name="interleave",
    )(mine, other)


def shift(value, axis, by):
    count = lax.axis_size(axis)
    return lax.ppermute(value, axis, [(one, (one + by) % count) for one in range(count)])


def swap(value, axis, bits, members=None):
    members = range(lax.axis_size(axis)) if members is None else members
    return lax.ppermute(value, axis, [(one, one ^ bits) for one in members])


def shards(
    visibilities, row_kernel, col_kernel, block_mask, tile_counts, tile_ids, tile_planes, w_values
):
    slots = tile_counts.shape[3]
    planes = w_values.shape[0]
    rows, vis_len = row_kernel.shape[4], row_kernel.shape[5]
    width = col_kernel.shape[5]
    img_count = lax.axis_size("img")
    wa_count = lax.axis_size("wa")
    full = rows * img_count
    table_r = jnp.asarray(row_table(NV // width, width), jnp.bfloat16)
    table_c = jnp.asarray(column_table(img_count, rows), jnp.bfloat16)
    own, send = gridding(
        tile_counts.reshape(slots),
        tile_ids.reshape(slots),
        tile_planes.reshape(slots),
        visibilities.reshape(2, slots, vis_len),
        block_mask.reshape(slots, -1, vis_len),
        row_kernel.reshape(slots, rows, vis_len),
        col_kernel.reshape(slots, vis_len, width),
        planes,
    )
    recv = shift(send, "blk", 1)
    groups = NV // 2 // LANES
    rotate = groups == img_count
    offsets = [3, 2, 0] if rotate else list(range(groups))
    neighbours = [0, 1] if rotate else [0]
    screen, middle, table_r, *columns = screens(
        offsets, neighbours, rotate, w_values, table_r, table_c
    )

    def over_wa(part):
        return [shift(part[by], "wa", by) for by in range(1, wa_count)]

    if rotate:
        outer, far, beside, here = first_images(
            [3, 2, 1, 0], 2, wa_count, own, recv, table_r, columns[0], screen, middle
        )
        from_beside = swap(beside, "img", 1)
        outer = add_rounded(outer[0], *over_wa(outer))
        far = add_rounded(far[0], *over_wa(far))
        from_outer = swap(outer, "img", 3)
        from_far = swap(far, "img", 2)
        (here,) = images(1, wa_count, 2, [here, from_beside], columns, screen, middle)
        total = add_up(here[0], *over_wa(here), from_outer, from_far)
    else:
        rowdft = row_transform(offsets, rotate, own, recv, table_r)
        parts = images(groups, wa_count, 0, rowdft, columns, screen, middle)
        part = jnp.stack(parts, axis=1)
        held = add_rounded(part[0], *over_wa(part))
        held = jnp.swapaxes(held, 0, 1).reshape(full // wa_count, img_count, -1)
        held = jnp.roll(jnp.swapaxes(held, 0, 1), -lax.axis_index("img"), axis=0)
        total = add_up(held[0], *(shift(held[by], "img", by) for by in range(1, img_count)))
    blk = lax.axis_index("blk")
    total = total.reshape(2, total.shape[0] // 2, total.shape[1])
    mine = lax.dynamic_index_in_dim(total, blk, 0, keepdims=False)
    other = lax.dynamic_index_in_dim(total, 1 - blk, 0, keepdims=False)
    other = shift(other.astype(jnp.bfloat16), "blk", 1)
    return interleave(mine, other, 1.0 / math.sqrt(full * NV * planes * wa_count))


def solution(mesh):
    in_specs = (
        P(None, ("parts", "img"), "wa", "blk", None, None),
        P(("parts", "img"), "wa", "blk", None, None, None),
        P(("parts", "img"), "wa", "blk", None, None, None),
        P(("parts", "img"), "wa", "blk", None, None, None),
        P(("parts", "img"), "wa", "blk", None),
        P(("parts", "img"), "wa", "blk", None),
        P(("parts", "img"), "wa", "blk", None),
        P(("parts", "wa")),
    )
    out_specs = P(("parts", "wa", "blk"), "img")
    return jax.shard_map(shards, mesh=mesh, in_specs=in_specs, out_specs=out_specs, check_vma=False)
```

```python
import functools
import math

import jax
import jax.numpy as jnp
import numpy as np
from jax import lax
from jax.experimental import pallas as pl
from jax.experimental.pallas import tpu as pltpu
from jax.sharding import PartitionSpec as P

NV = 1024
LANES = 128
VMEM = pltpu.VMEM
SMEM = pltpu.SMEM
HBM = pltpu.HBM


def angles(first, second, length):
    return 2.0 * np.pi / length * (np.outer(first, second) % length)


def row_table(across, tile_width):
    half_v = np.arange(NV // 2)
    out = []
    for parity in range(2):
        m_index = 2 * np.arange(NV // 2) + parity
        ang = angles(half_v, m_index, NV)
        cosine, sine = np.cos(ang), np.sin(ang)
        real = np.stack([cosine, -sine])
        imag = np.stack([sine, cosine])
        both = np.stack([real, imag])
        both = both.reshape(2, 2, across // 2, tile_width, NV // 2 // LANES, LANES)
        out.append(both.transpose(4, 2, 1, 3, 0, 5).reshape(-1, NV, 2 * LANES))
    return np.stack(out)


def column_table(img_count, rows):
    full = img_count * rows
    ang = angles(np.arange(full // 2), np.arange(full), full)
    cosine, sine = np.cos(ang), np.sin(ang)
    sine[0] = np.cos(np.pi * (np.arange(full) % 2))
    both = np.stack([cosine, sine]).reshape(2, full // 2, img_count, rows)
    return both.transpose(2, 0, 1, 3)


def grid_kernel(
    counts_hbm,
    ids_hbm,
    planes_hbm,
    vis_hbm,
    mask_hbm,
    rk_hbm,
    ck_hbm,
    own_ref,
    send_ref,
    counts_ref,
    ids_ref,
    planes_ref,
    vis_ref,
    mask_ref,
    rk_ref,
    ck_ref,
    acc,
    small_sem,
    rk_sem,
    ck_sem,
):
    blk = lax.axis_index("blk")
    slots, rows, vis_len = rk_ref.shape
    codes = acc.shape[0]
    width = ck_ref.shape[2]
    blocks = mask_ref.shape[1]
    planes = own_ref.shape[0]
    across = codes // planes
    chunks = rk_sem.shape[0]
    group = slots // chunks

    small = [
        pltpu.make_async_copy(source, target, small_sem.at[n])
        for n, (source, target) in enumerate(
            [
                (counts_hbm, counts_ref),
                (ids_hbm, ids_ref),
                (planes_hbm, planes_ref),
                (vis_hbm, vis_ref),
                (mask_hbm, mask_ref),
            ]
        )
    ]
    cols_copy = pltpu.make_async_copy(ck_hbm, ck_ref, ck_sem.at[0])
    large = []
    for n in range(chunks):
        part = pl.ds(n * group, group)
        large.append(pltpu.make_async_copy(rk_hbm.at[part], rk_ref.at[part], rk_sem.at[n]))
    for copy in [*small, cols_copy, *large]:
        copy.start()
    acc[...] = jnp.zeros_like(acc)
    for copy in small:
        copy.wait()

    lane = lax.broadcasted_iota(jnp.int32, (1, vis_len), 1)
    real, imag = [], []
    for slot in range(slots):
        mask = mask_ref[slot].astype(jnp.float32) * (lane < counts_ref[slot]).astype(jnp.float32)
        real.append(mask * vis_ref[0, pl.ds(slot, 1), :].astype(jnp.float32))
        imag.append(mask * vis_ref[1, pl.ds(slot, 1), :].astype(jnp.float32))
    scaled = [jnp.concatenate(value, axis=0).T for value in (real, imag)]
    block_of = lax.broadcasted_iota(jnp.int32, (vis_len, width), 1) // (width // blocks)
    per = width // blocks
    for slot in range(slots):
        if slot == 0:
            cols_copy.wait()
        if slot % group == 0:
            large[slot // group].wait()
        here = slice(slot // per * width, (slot // per + 1) * width)
        source = block_of + slot % per * blocks
        weighted = jnp.concatenate(
            [
                jnp.take_along_axis(value[:, here], source, axis=1).astype(jnp.bfloat16)
                * ck_ref[slot]
                for value in scaled
            ],
            axis=1,
        )
        tile = jnp.dot(rk_ref[slot], weighted, preferred_element_type=jnp.float32)
        acc[planes_ref[slot] * across + ids_ref[slot]] += tile

    sign = (1 - 2 * blk).astype(jnp.float32)
    for plane in range(planes):
        for t in range(across // 2):
            low = acc[plane * across + t]
            high = acc[plane * across + t + across // 2] * sign
            where = pl.ds(t * 2 * width, 2 * width)
            own_ref[plane, :, where] = (low + high).astype(jnp.bfloat16)
            send_ref[plane, :, where] = (low - high).astype(jnp.bfloat16)


def gridding(counts, ids, levels, vis, mask, rk, ck, planes):
    slots, rows, vis_len = rk.shape
    width = ck.shape[2]
    across = NV // width
    chunks = 2
    half = (planes, rows, NV)
    inputs = (counts, ids, levels, vis, mask, rk, ck)
    return pl.pallas_call(
        grid_kernel,
        in_specs=[pl.BlockSpec(memory_space=HBM)] * len(inputs),
        out_specs=[pl.BlockSpec(memory_space=VMEM)] * 2,
        out_shape=[jax.ShapeDtypeStruct(half, jnp.bfloat16)] * 2,
        scratch_shapes=[SMEM(counts.shape, jnp.int32)] * 3
        + [VMEM(value.shape, value.dtype) for value in (vis, mask, rk, ck)]
        + [
            VMEM((planes * across, rows, 2 * width), jnp.float32),
            pltpu.SemaphoreType.DMA((5,)),
            pltpu.SemaphoreType.DMA((chunks,)),
            pltpu.SemaphoreType.DMA((1,)),
        ],
        compiler_params=pltpu.CompilerParams(vmem_limit_bytes=24 << 20),
        name="gridding",
    )(*(pltpu.with_memory_space_constraint(value, HBM) for value in inputs))


COS_POLY = np.polynomial.chebyshev.Chebyshev.interpolate(
    lambda z: np.cos(2 * np.pi * np.sqrt(np.maximum(z, 0.0))), 5, [0.0, 0.25]
).convert(kind=np.polynomial.Polynomial).coef
SIN_POLY = np.polynomial.chebyshev.Chebyshev.interpolate(
    lambda z: np.sinc(2 * np.sqrt(np.maximum(z, 0.0))) * 2 * np.pi, 5, [0.0, 0.25]
).convert(kind=np.polynomial.Polynomial).coef


def horner(coef, z):
    total = jnp.full_like(z, float(coef[-1]))
    for value in coef[-2::-1]:
        total = total * z + float(value)
    return total


def turn(cycles):
    rest = cycles - jnp.round(cycles)
    square = rest * rest
    return horner(COS_POLY, square), horner(SIN_POLY, square) * rest


def screen_kernel(
    offsets, neighbours, rotate, w_ref, table_r_hbm, table_c_hbm, screen_ref, middle_ref, table_r_ref, *refs
):
    columns, sem = refs[:-1], refs[-1]
    img = lax.axis_index("img")
    copies = [pltpu.make_async_copy(table_r_hbm.at[lax.axis_index("blk")], table_r_ref, sem.at[0])]
    for n, ref in enumerate(columns):
        source = table_c_hbm.at[img ^ neighbours[n]]
        copies.append(pltpu.make_async_copy(source, ref, sem.at[1 + n]))
    for copy in copies:
        copy.start()
    planes, _, half, _ = screen_ref.shape
    full = 2 * half
    blk = lax.axis_index("blk")
    block = LANES
    for n, k in enumerate(offsets):
        g = lax.axis_index("img") ^ k if rotate else k
        column = 2 * (g * LANES + lax.broadcasted_iota(jnp.int32, (1, LANES), 1)) + blk
        y = (column.astype(jnp.float32) - NV / 2) / NV
        rest_y = 1.0 - y * y
        for q in range(planes):
            cosine, sine = turn((jnp.sqrt(rest_y) - 1.0) * w_ref[q])
            middle_ref[q, n] = jnp.concatenate([cosine, sine], axis=1)
        for start in range(0, half, block):
            row = start + lax.broadcasted_iota(jnp.int32, (block, 1), 0)
            x = (row.astype(jnp.float32) - half) / full
            nterm = jnp.sqrt(rest_y - x * x) - 1.0
            for q in range(planes):
                cosine, sine = turn(nterm * w_ref[q])
                screen_ref[q, n, start : start + block, :LANES] = cosine
                screen_ref[q, n, start : start + block, LANES:] = sine
    for copy in copies:
        copy.wait()


def screens(offsets, neighbours, rotate, w_values, table_r, table_c):
    planes = w_values.shape[0]
    groups, n_columns = len(offsets), len(neighbours)
    half = table_c.shape[2]
    tables = [pltpu.with_memory_space_constraint(value, HBM) for value in (table_r, table_c)]
    return pl.pallas_call(
        functools.partial(screen_kernel, offsets, neighbours, rotate),
        in_specs=[pl.BlockSpec(memory_space=SMEM)] + [pl.BlockSpec(memory_space=HBM)] * 2,
        out_specs=[pl.BlockSpec(memory_space=VMEM)] * (3 + n_columns),
        out_shape=[
            jax.ShapeDtypeStruct((planes, groups, half, 2 * LANES), jnp.float32),
            jax.ShapeDtypeStruct((planes, groups, 1, 2 * LANES), jnp.float32),
            jax.ShapeDtypeStruct(table_r.shape[1:], jnp.bfloat16),
        ]
        + [jax.ShapeDtypeStruct(table_c.shape[1:], jnp.bfloat16)] * n_columns,
        scratch_shapes=[pltpu.SemaphoreType.DMA((1 + n_columns,))],
        compiler_params=pltpu.CompilerParams(vmem_limit_bytes=24 << 20),
        cost_estimate=pl.CostEstimate(
            flops=planes * half * NV * 20, bytes_accessed=planes * half * NV * 4, transcendentals=0
        ),
        name="screens",
    )(w_values, *tables)


def row_kernel_body(offsets, rotate, own_ref, recv_ref, table_r, *outs):
    planes, rows, _ = own_ref.shape
    groups = table_r.shape[0]
    grid = (own_ref[...] + recv_ref[...]).reshape(planes * rows, NV)
    for out_ref, k in zip(outs, offsets):
        g = lax.axis_index("img") ^ k if rotate else k
        out_ref[...] = jnp.dot(grid, table_r[g], preferred_element_type=jnp.float32).astype(
            jnp.bfloat16
        )


def row_transform(offsets, rotate, own, recv, table_r):
    planes, rows, _ = own.shape
    one = jax.ShapeDtypeStruct((planes * rows, 2 * LANES), jnp.bfloat16)
    return pl.pallas_call(
        functools.partial(row_kernel_body, offsets, rotate),
        in_specs=[pl.BlockSpec(memory_space=VMEM)] * 3,
        out_specs=[pl.BlockSpec(memory_space=VMEM)] * len(offsets),
        out_shape=[one] * len(offsets),
        compiler_params=pltpu.CompilerParams(vmem_limit_bytes=24 << 20),
        name="row_dft",
    )(own, recv, table_r)


def image_kernel(count, depth, first_screen, *refs):
    rowdft = refs[: count * depth]
    tables = refs[count * depth : (count + 1) * depth]
    screen_ref, middle_ref, *outs, back = refs[(count + 1) * depth :]
    planes = screen_ref.shape[0]
    rows = rowdft[0].shape[0] // planes
    wa = lax.axis_index("wa")
    wa_count, piece = outs[0].shape[0], outs[0].shape[1]
    half = tables[0].shape[1]
    block = LANES
    row_at = lax.broadcasted_iota(jnp.int32, (block, block), 0)
    col_at = lax.broadcasted_iota(jnp.int32, (block, block), 1)
    flip = (row_at + col_at == block).astype(jnp.bfloat16)
    top = lax.broadcasted_iota(jnp.int32, (block, 1), 0) == 0

    def put(start, count, n, value):
        for j in range(count // piece):
            at = lax.rem(start // piece + j - wa + wa_count, wa_count)
            outs[n][at] = value[j * piece : (j + 1) * piece]

    for n in range(count):
        at_screen = first_screen + n
        firsts = []
        for start in range(0, half, block):
            even = jnp.zeros((block, LANES), jnp.float32)
            odd = jnp.zeros((block, LANES), jnp.float32)
            for q in range(planes):
                by_cos, by_sin = (
                    sum(
                        jnp.dot(
                            tables[d][which, start : start + block],
                            rowdft[n * depth + d][q * rows : (q + 1) * rows],
                            preferred_element_type=jnp.float32,
                        )
                        for d in range(depth)
                    )
                    for which in range(2)
                )
                cosine = screen_ref[q, at_screen, start : start + block, :LANES]
                sine = screen_ref[q, at_screen, start : start + block, LANES:]
                even += cosine * by_cos[:, :LANES] - sine * by_cos[:, LANES:]
                if start == 0:
                    row = lax.broadcasted_iota(jnp.int32, (block, 1), 0)
                    cosine, sine = (
                        jnp.where(row == 0, -middle_ref[q, at_screen, :, LANES:], cosine),
                        jnp.where(row == 0, middle_ref[q, at_screen, :, :LANES], sine),
                    )
                odd += cosine * by_sin[:, LANES:] + sine * by_sin[:, :LANES]
            low, high = even - odd, even + odd
            if start == 0:
                low = jnp.where(row == 0, even, low)
                high = jnp.where(row == 0, odd, high)
            firsts.append(low.astype(jnp.bfloat16))
            back[start : start + block] = high.astype(jnp.bfloat16)
        put(0, half, n, jnp.concatenate(firsts, axis=0))
        seconds = []
        for start in range(0, half, block):
            mirror = half - block - start
            first = back[pl.ds((half - start) % half, 16), :][:1].astype(jnp.float32)
            rest = jnp.dot(flip, back[mirror : mirror + block], preferred_element_type=jnp.float32)
            seconds.append(jnp.where(top, first, rest).astype(jnp.bfloat16))
        put(half, half, n, jnp.concatenate(seconds, axis=0))


def first_kernel(offsets, own_ref, recv_ref, table_r, table_c, screen_ref, middle_ref, *refs):
    *outs, rowdft, back = refs
    count = rowdft.shape[0]
    blocks = [rowdft.at[n] for n in range(count)]
    row_kernel_body(offsets, True, own_ref, recv_ref, table_r, *blocks, *outs[count:])
    image_kernel(count, 1, 0, *blocks, table_c, screen_ref, middle_ref, *outs[:count], back)


def first_images(offsets, count, wa_count, own, recv, table_r, table_c, screen, middle):
    half = table_c.shape[1]
    planes, rows, _ = own.shape
    inputs = (own, recv, table_r, table_c, screen, middle)
    image = jax.ShapeDtypeStruct((wa_count, 2 * half // wa_count, LANES), jnp.bfloat16)
    block = jax.ShapeDtypeStruct((planes * rows, 2 * LANES), jnp.bfloat16)
    return pl.pallas_call(
        functools.partial(first_kernel, offsets),
        in_specs=[pl.BlockSpec(memory_space=VMEM)] * len(inputs),
        out_specs=[pl.BlockSpec(memory_space=VMEM)] * len(offsets),
        out_shape=[image] * count + [block] * (len(offsets) - count),
        scratch_shapes=[
            VMEM((count, planes * rows, 2 * LANES), jnp.bfloat16),
            VMEM((half, LANES), jnp.bfloat16),
        ],
        compiler_params=pltpu.CompilerParams(vmem_limit_bytes=24 << 20),
        name="first_images",
    )(*inputs)


def images(count, wa_count, first_screen, rowdft, tables, screen, middle):
    half = tables[0].shape[1]
    inputs = (*rowdft, *tables, screen, middle)
    one = jax.ShapeDtypeStruct((wa_count, 2 * half // wa_count, LANES), jnp.bfloat16)
    return pl.pallas_call(
        functools.partial(image_kernel, count, len(tables), first_screen),
        in_specs=[pl.BlockSpec(memory_space=VMEM)] * len(inputs),
        out_specs=[pl.BlockSpec(memory_space=VMEM)] * count,
        out_shape=[one] * count,
        scratch_shapes=[VMEM((half, LANES), jnp.bfloat16)],
        compiler_params=pltpu.CompilerParams(vmem_limit_bytes=24 << 20),
        name=f"image_{count}_{len(tables)}",
    )(*inputs)


def add_kernel(one_ref, *refs):
    total = one_ref[...].astype(jnp.float32)
    for ref in refs[:-1]:
        total += ref[...].astype(jnp.float32)
    refs[-1][...] = total.astype(refs[-1].dtype)


def add_rounded(*parts):
    return pl.pallas_call(
        add_kernel,
        in_specs=[pl.BlockSpec(memory_space=VMEM)] * len(parts),
        out_specs=pl.BlockSpec(memory_space=VMEM),
        out_shape=jax.ShapeDtypeStruct(parts[0].shape, jnp.bfloat16),
        compiler_params=pltpu.CompilerParams(vmem_limit_bytes=24 << 20),
        name="add",
    )(*parts)


def add_up(*parts):
    return sum(part.astype(jnp.float32) for part in parts)


def final_kernel(scale, mine_ref, other_ref, out_ref):
    blk = lax.axis_index("blk")
    count = mine_ref.shape[1]
    source = lax.broadcasted_iota(jnp.int32, (2 * count, 2 * count), 0)
    target = lax.broadcasted_iota(jnp.int32, (2 * count, 2 * count), 1)
    wanted = jnp.where(source < count, 2 * source + blk, 2 * (source - count) + 1 - blk)
    place = (wanted == target).astype(jnp.bfloat16)
    rest = jnp.concatenate([mine_ref[...], other_ref[...].astype(jnp.float32)], axis=1) * scale
    total = jnp.zeros(out_ref.shape, jnp.float32)
    for _ in range(2):
        term = rest.astype(jnp.bfloat16)
        total += jnp.dot(term, place, preferred_element_type=jnp.float32)
        rest = rest - term.astype(jnp.float32)
    out_ref[...] = total


def interleave(mine, other, scale):
    return pl.pallas_call(
        functools.partial(final_kernel, scale),
        in_specs=[pl.BlockSpec(memory_space=VMEM)] * 2,
        out_specs=pl.BlockSpec(memory_space=VMEM),
        out_shape=jax.ShapeDtypeStruct((mine.shape[0], 2 * mine.shape[1]), jnp.float32),
        compiler_params=pltpu.CompilerParams(vmem_limit_bytes=24 << 20),
        name="interleave",
    )(mine, other)


def shift(value, axis, by):
    count = lax.axis_size(axis)
    return lax.ppermute(value, axis, [(one, (one + by) % count) for one in range(count)])


def swap(value, axis, bits, members=None):
    members = range(lax.axis_size(axis)) if members is None else members
    return lax.ppermute(value, axis, [(one, one ^ bits) for one in members])


def shards(
    visibilities, row_kernel, col_kernel, block_mask, tile_counts, tile_ids, tile_planes, w_values
):
    slots = tile_counts.shape[3]
    planes = w_values.shape[0]
    rows, vis_len = row_kernel.shape[4], row_kernel.shape[5]
    width = col_kernel.shape[5]
    img_count = lax.axis_size("img")
    wa_count = lax.axis_size("wa")
    full = rows * img_count
    table_r = jnp.asarray(row_table(NV // width, width), jnp.bfloat16)
    table_c = jnp.asarray(column_table(img_count, rows), jnp.bfloat16)
    own, send = gridding(
        tile_counts.reshape(slots),
        tile_ids.reshape(slots),
        tile_planes.reshape(slots),
        visibilities.reshape(2, slots, vis_len),
        block_mask.reshape(slots, -1, vis_len),
        row_kernel.reshape(slots, rows, vis_len),
        col_kernel.reshape(slots, vis_len, width),
        planes,
    )
    recv = shift(send, "blk", 1)
    groups = NV // 2 // LANES
    rotate = groups == img_count
    offsets = [3, 2, 0] if rotate else list(range(groups))
    neighbours = [0, 1] if rotate else [0]
    screen, middle, table_r, *columns = screens(
        offsets, neighbours, rotate, w_values, table_r, table_c
    )

    def over_wa(part):
        return [shift(part[by], "wa", by) for by in range(1, wa_count)]

    if rotate:
        outer, far, beside, here = first_images(
            [3, 2, 1, 0], 2, wa_count, own, recv, table_r, columns[0], screen, middle
        )
        from_beside = swap(beside, "img", 1)
        outer = add_rounded(outer[0], *over_wa(outer))
        far = add_rounded(far[0], *over_wa(far))
        from_outer = swap(outer, "img", 3)
        from_far = swap(far, "img", 2)
        (here,) = images(1, wa_count, 2, [here, from_beside], columns, screen, middle)
        total = add_up(here[0], *over_wa(here), from_outer, from_far)
    else:
        rowdft = row_transform(offsets, rotate, own, recv, table_r)
        parts = images(groups, wa_count, 0, rowdft, columns, screen, middle)
        part = jnp.stack(parts, axis=1)
        held = add_rounded(part[0], *over_wa(part))
        held = jnp.swapaxes(held, 0, 1).reshape(full // wa_count, img_count, -1)
        held = jnp.roll(jnp.swapaxes(held, 0, 1), -lax.axis_index("img"), axis=0)
        total = add_up(held[0], *(shift(held[by], "img", by) for by in range(1, img_count)))
    blk = lax.axis_index("blk")
    total = total.reshape(2, total.shape[0] // 2, total.shape[1])
    mine = lax.dynamic_index_in_dim(total, blk, 0, keepdims=False)
    other = lax.dynamic_index_in_dim(total, 1 - blk, 0, keepdims=False)
    other = shift(other.astype(jnp.bfloat16), "blk", 1)
    return interleave(mine, other, 1.0 / math.sqrt(full * NV * planes * wa_count))


def solution(mesh):
    in_specs = (
        P(None, ("parts", "img"), "wa", "blk", None, None),
        P(("parts", "img"), "wa", "blk", None, None, None),
        P(("parts", "img"), "wa", "blk", None, None, None),
        P(("parts", "img"), "wa", "blk", None, None, None),
        P(("parts", "img"), "wa", "blk", None),
        P(("parts", "img"), "wa", "blk", None),
        P(("parts", "img"), "wa", "blk", None),
        P(("parts", "wa")),
    )
    out_specs = P(("parts", "wa", "blk"), "img")
    return jax.shard_map(shards, mesh=mesh, in_specs=in_specs, out_specs=out_specs, check_vma=False)
```

```python
import functools
import math

import jax
import jax.numpy as jnp
import numpy as np
from jax import lax
from jax.experimental import pallas as pl
from jax.experimental.pallas import tpu as pltpu
from jax.sharding import PartitionSpec as P

NV = 1024
LANES = 128
VMEM = pltpu.VMEM
SMEM = pltpu.SMEM
HBM = pltpu.HBM


def angles(first, second, length):
    return 2.0 * np.pi / length * (np.outer(first, second) % length)


def row_table(across, tile_width):
    half_v = np.arange(NV // 2)
    out = []
    for parity in range(2):
        m_index = 2 * np.arange(NV // 2) + parity
        ang = angles(half_v, m_index, NV)
        cosine, sine = np.cos(ang), np.sin(ang)
        real = np.stack([cosine, -sine])
        imag = np.stack([sine, cosine])
        both = np.stack([real, imag])
        both = both.reshape(2, 2, across // 2, tile_width, NV // 2 // LANES, LANES)
        out.append(both.transpose(4, 2, 1, 3, 0, 5).reshape(-1, NV, 2 * LANES))
    return np.stack(out)


def column_table(img_count, rows):
    full = img_count * rows
    ang = angles(np.arange(full // 2), np.arange(full), full)
    cosine, sine = np.cos(ang), np.sin(ang)
    sine[0] = np.cos(np.pi * (np.arange(full) % 2))
    both = np.stack([cosine, sine]).reshape(2, full // 2, img_count, rows)
    return both.transpose(2, 0, 1, 3)


def grid_kernel(
    counts_hbm,
    ids_hbm,
    planes_hbm,
    vis_hbm,
    mask_hbm,
    rk_hbm,
    ck_hbm,
    own_ref,
    send_ref,
    counts_ref,
    ids_ref,
    planes_ref,
    vis_ref,
    mask_ref,
    rk_ref,
    ck_ref,
    acc,
    small_sem,
    rk_sem,
    ck_sem,
):
    blk = lax.axis_index("blk")
    slots, rows, vis_len = rk_ref.shape
    codes = acc.shape[0]
    width = ck_ref.shape[2]
    blocks = mask_ref.shape[1]
    planes = own_ref.shape[0]
    across = codes // planes
    chunks = rk_sem.shape[0]
    group = slots // chunks

    small = [
        pltpu.make_async_copy(source, target, small_sem.at[n])
        for n, (source, target) in enumerate(
            [
                (counts_hbm, counts_ref),
                (ids_hbm, ids_ref),
                (planes_hbm, planes_ref),
                (vis_hbm, vis_ref),
                (mask_hbm, mask_ref),
            ]
        )
    ]
    cols_copy = pltpu.make_async_copy(ck_hbm, ck_ref, ck_sem.at[0])
    large = []
    for n in range(chunks):
        part = pl.ds(n * group, group)
        large.append(pltpu.make_async_copy(rk_hbm.at[part], rk_ref.at[part], rk_sem.at[n]))
    for copy in [large[0], *small, cols_copy, *large[1:]]:
        copy.start()
    acc[...] = jnp.zeros_like(acc)
    for copy in small:
        copy.wait()

    lane = lax.broadcasted_iota(jnp.int32, (1, vis_len), 1)
    real, imag = [], []
    for slot in range(slots):
        mask = mask_ref[slot].astype(jnp.float32) * (lane < counts_ref[slot]).astype(jnp.float32)
        real.append(mask * vis_ref[0, pl.ds(slot, 1), :].astype(jnp.float32))
        imag.append(mask * vis_ref[1, pl.ds(slot, 1), :].astype(jnp.float32))
    scaled = [jnp.concatenate(value, axis=0).T for value in (real, imag)]
    block_of = lax.broadcasted_iota(jnp.int32, (vis_len, width), 1) // (width // blocks)
    per = width // blocks
    for slot in range(slots):
        if slot == 0:
            cols_copy.wait()
        if slot % group == 0:
            large[slot // group].wait()
        here = slice(slot // per * width, (slot // per + 1) * width)
        source = block_of + slot % per * blocks
        weighted = jnp.concatenate(
            [
                jnp.take_along_axis(value[:, here], source, axis=1).astype(jnp.bfloat16)
                * ck_ref[slot]
                for value in scaled
            ],
            axis=1,
        )
        tile = jnp.dot(rk_ref[slot], weighted, preferred_element_type=jnp.float32)
        acc[planes_ref[slot] * across + ids_ref[slot]] += tile

    sign = (1 - 2 * blk).astype(jnp.float32)
    for plane in range(planes):
        for t in range(across // 2):
            low = acc[plane * across + t]
            high = acc[plane * across + t + across // 2] * sign
            where = pl.ds(t * 2 * width, 2 * width)
            own_ref[plane, :, where] = (low + high).astype(jnp.bfloat16)
            send_ref[plane, :, where] = (low - high).astype(jnp.bfloat16)


def gridding(counts, ids, levels, vis, mask, rk, ck, planes):
    slots, rows, vis_len = rk.shape
    width = ck.shape[2]
    across = NV // width
    chunks = 2
    half = (planes, rows, NV)
    inputs = (counts, ids, levels, vis, mask, rk, ck)
    return pl.pallas_call(
        grid_kernel,
        in_specs=[pl.BlockSpec(memory_space=HBM)] * len(inputs),
        out_specs=[pl.BlockSpec(memory_space=VMEM)] * 2,
        out_shape=[jax.ShapeDtypeStruct(half, jnp.bfloat16)] * 2,
        scratch_shapes=[SMEM(counts.shape, jnp.int32)] * 3
        + [VMEM(value.shape, value.dtype) for value in (vis, mask, rk, ck)]
        + [
            VMEM((planes * across, rows, 2 * width), jnp.float32),
            pltpu.SemaphoreType.DMA((5,)),
            pltpu.SemaphoreType.DMA((chunks,)),
            pltpu.SemaphoreType.DMA((1,)),
        ],
        compiler_params=pltpu.CompilerParams(vmem_limit_bytes=24 << 20),
        name="gridding",
    )(*(pltpu.with_memory_space_constraint(value, HBM) for value in inputs))


COS_POLY = np.polynomial.chebyshev.Chebyshev.interpolate(
    lambda z: np.cos(2 * np.pi * np.sqrt(np.maximum(z, 0.0))), 5, [0.0, 0.25]
).convert(kind=np.polynomial.Polynomial).coef
SIN_POLY = np.polynomial.chebyshev.Chebyshev.interpolate(
    lambda z: np.sinc(2 * np.sqrt(np.maximum(z, 0.0))) * 2 * np.pi, 5, [0.0, 0.25]
).convert(kind=np.polynomial.Polynomial).coef


def horner(coef, z):
    total = jnp.full_like(z, float(coef[-1]))
    for value in coef[-2::-1]:
        total = total * z + float(value)
    return total


def turn(cycles):
    rest = cycles - jnp.round(cycles)
    square = rest * rest
    return horner(COS_POLY, square), horner(SIN_POLY, square) * rest


def screen_kernel(
    offsets, neighbours, rotate, w_ref, table_r_hbm, table_c_hbm, screen_ref, middle_ref, table_r_ref, *refs
):
    columns, sem = refs[:-1], refs[-1]
    img = lax.axis_index("img")
    copies = [pltpu.make_async_copy(table_r_hbm.at[lax.axis_index("blk")], table_r_ref, sem.at[0])]
    for n, ref in enumerate(columns):
        source = table_c_hbm.at[img ^ neighbours[n]]
        copies.append(pltpu.make_async_copy(source, ref, sem.at[1 + n]))
    for copy in copies:
        copy.start()
    planes, _, half, _ = screen_ref.shape
    full = 2 * half
    blk = lax.axis_index("blk")
    block = LANES
    for n, k in enumerate(offsets):
        g = lax.axis_index("img") ^ k if rotate else k
        column = 2 * (g * LANES + lax.broadcasted_iota(jnp.int32, (1, LANES), 1)) + blk
        y = (column.astype(jnp.float32) - NV / 2) / NV
        rest_y = 1.0 - y * y
        for q in range(planes):
            cosine, sine = turn((jnp.sqrt(rest_y) - 1.0) * w_ref[q])
            middle_ref[q, n] = jnp.concatenate([cosine, sine], axis=1)
        for start in range(0, half, block):
            row = start + lax.broadcasted_iota(jnp.int32, (block, 1), 0)
            x = (row.astype(jnp.float32) - half) / full
            nterm = jnp.sqrt(rest_y - x * x) - 1.0
            for q in range(planes):
                cosine, sine = turn(nterm * w_ref[q])
                screen_ref[q, n, start : start + block, :LANES] = cosine
                screen_ref[q, n, start : start + block, LANES:] = sine
    for copy in copies:
        copy.wait()


def screens(offsets, neighbours, rotate, w_values, table_r, table_c):
    planes = w_values.shape[0]
    groups, n_columns = len(offsets), len(neighbours)
    half = table_c.shape[2]
    tables = [pltpu.with_memory_space_constraint(value, HBM) for value in (table_r, table_c)]
    return pl.pallas_call(
        functools.partial(screen_kernel, offsets, neighbours, rotate),
        in_specs=[pl.BlockSpec(memory_space=SMEM)] + [pl.BlockSpec(memory_space=HBM)] * 2,
        out_specs=[pl.BlockSpec(memory_space=VMEM)] * (3 + n_columns),
        out_shape=[
            jax.ShapeDtypeStruct((planes, groups, half, 2 * LANES), jnp.float32),
            jax.ShapeDtypeStruct((planes, groups, 1, 2 * LANES), jnp.float32),
            jax.ShapeDtypeStruct(table_r.shape[1:], jnp.bfloat16),
        ]
        + [jax.ShapeDtypeStruct(table_c.shape[1:], jnp.bfloat16)] * n_columns,
        scratch_shapes=[pltpu.SemaphoreType.DMA((1 + n_columns,))],
        compiler_params=pltpu.CompilerParams(vmem_limit_bytes=24 << 20),
        cost_estimate=pl.CostEstimate(
            flops=planes * half * NV * 20, bytes_accessed=planes * half * NV * 4, transcendentals=0
        ),
        name="screens",
    )(w_values, *tables)


def row_kernel_body(offsets, rotate, own_ref, recv_ref, table_r, *outs):
    planes, rows, _ = own_ref.shape
    groups = table_r.shape[0]
    grid = (own_ref[...] + recv_ref[...]).reshape(planes * rows, NV)
    for out_ref, k in zip(outs, offsets):
        g = lax.axis_index("img") ^ k if rotate else k
        out_ref[...] = jnp.dot(grid, table_r[g], preferred_element_type=jnp.float32).astype(
            jnp.bfloat16
        )


def row_transform(offsets, rotate, own, recv, table_r):
    planes, rows, _ = own.shape
    one = jax.ShapeDtypeStruct((planes * rows, 2 * LANES), jnp.bfloat16)
    return pl.pallas_call(
        functools.partial(row_kernel_body, offsets, rotate),
        in_specs=[pl.BlockSpec(memory_space=VMEM)] * 3,
        out_specs=[pl.BlockSpec(memory_space=VMEM)] * len(offsets),
        out_shape=[one] * len(offsets),
        compiler_params=pltpu.CompilerParams(vmem_limit_bytes=24 << 20),
        name="row_dft",
    )(own, recv, table_r)


def image_kernel(count, depth, first_screen, *refs):
    rowdft = refs[: count * depth]
    tables = refs[count * depth : (count + 1) * depth]
    screen_ref, middle_ref, *outs, back = refs[(count + 1) * depth :]
    planes = screen_ref.shape[0]
    rows = rowdft[0].shape[0] // planes
    wa = lax.axis_index("wa")
    wa_count, piece = outs[0].shape[0], outs[0].shape[1]
    half = tables[0].shape[1]
    block = LANES
    row_at = lax.broadcasted_iota(jnp.int32, (block, block), 0)
    col_at = lax.broadcasted_iota(jnp.int32, (block, block), 1)
    flip = (row_at + col_at == block).astype(jnp.bfloat16)
    top = lax.broadcasted_iota(jnp.int32, (block, 1), 0) == 0

    def put(start, count, n, value):
        for j in range(count // piece):
            at = lax.rem(start // piece + j - wa + wa_count, wa_count)
            outs[n][at] = value[j * piece : (j + 1) * piece]

    for n in range(count):
        at_screen = first_screen + n
        firsts = []
        for start in range(0, half, block):
            even = jnp.zeros((block, LANES), jnp.float32)
            odd = jnp.zeros((block, LANES), jnp.float32)
            for q in range(planes):
                by_cos, by_sin = (
                    sum(
                        jnp.dot(
                            tables[d][which, start : start + block],
                            rowdft[n * depth + d][q * rows : (q + 1) * rows],
                            preferred_element_type=jnp.float32,
                        )
                        for d in range(depth)
                    )
                    for which in range(2)
                )
                cosine = screen_ref[q, at_screen, start : start + block, :LANES]
                sine = screen_ref[q, at_screen, start : start + block, LANES:]
                even += cosine * by_cos[:, :LANES] - sine * by_cos[:, LANES:]
                if start == 0:
                    row = lax.broadcasted_iota(jnp.int32, (block, 1), 0)
                    cosine, sine = (
                        jnp.where(row == 0, -middle_ref[q, at_screen, :, LANES:], cosine),
                        jnp.where(row == 0, middle_ref[q, at_screen, :, :LANES], sine),
                    )
                odd += cosine * by_sin[:, LANES:] + sine * by_sin[:, :LANES]
            low, high = even - odd, even + odd
            if start == 0:
                low = jnp.where(row == 0, even, low)
                high = jnp.where(row == 0, odd, high)
            firsts.append(low.astype(jnp.bfloat16))
            back[start : start + block] = high.astype(jnp.bfloat16)
        put(0, half, n, jnp.concatenate(firsts, axis=0))
        seconds = []
        for start in range(0, half, block):
            mirror = half - block - start
            first = back[pl.ds((half - start) % half, 16), :][:1].astype(jnp.float32)
            rest = jnp.dot(flip, back[mirror : mirror + block], preferred_element_type=jnp.float32)
            seconds.append(jnp.where(top, first, rest).astype(jnp.bfloat16))
        put(half, half, n, jnp.concatenate(seconds, axis=0))


def first_kernel(offsets, own_ref, recv_ref, table_r, table_c, screen_ref, middle_ref, *refs):
    *outs, rowdft, back = refs
    count = rowdft.shape[0]
    blocks = [rowdft.at[n] for n in range(count)]
    row_kernel_body(offsets, True, own_ref, recv_ref, table_r, *blocks, *outs[count:])
    image_kernel(count, 1, 0, *blocks, table_c, screen_ref, middle_ref, *outs[:count], back)


def first_images(offsets, count, wa_count, own, recv, table_r, table_c, screen, middle):
    half = table_c.shape[1]
    planes, rows, _ = own.shape
    inputs = (own, recv, table_r, table_c, screen, middle)
    image = jax.ShapeDtypeStruct((wa_count, 2 * half // wa_count, LANES), jnp.bfloat16)
    block = jax.ShapeDtypeStruct((planes * rows, 2 * LANES), jnp.bfloat16)
    return pl.pallas_call(
        functools.partial(first_kernel, offsets),
        in_specs=[pl.BlockSpec(memory_space=VMEM)] * len(inputs),
        out_specs=[pl.BlockSpec(memory_space=VMEM)] * len(offsets),
        out_shape=[image] * count + [block] * (len(offsets) - count),
        scratch_shapes=[
            VMEM((count, planes * rows, 2 * LANES), jnp.bfloat16),
            VMEM((half, LANES), jnp.bfloat16),
        ],
        compiler_params=pltpu.CompilerParams(vmem_limit_bytes=24 << 20),
        name="first_images",
    )(*inputs)


def images(count, wa_count, first_screen, rowdft, tables, screen, middle):
    half = tables[0].shape[1]
    inputs = (*rowdft, *tables, screen, middle)
    one = jax.ShapeDtypeStruct((wa_count, 2 * half // wa_count, LANES), jnp.bfloat16)
    return pl.pallas_call(
        functools.partial(image_kernel, count, len(tables), first_screen),
        in_specs=[pl.BlockSpec(memory_space=VMEM)] * len(inputs),
        out_specs=[pl.BlockSpec(memory_space=VMEM)] * count,
        out_shape=[one] * count,
        scratch_shapes=[VMEM((half, LANES), jnp.bfloat16)],
        compiler_params=pltpu.CompilerParams(vmem_limit_bytes=24 << 20),
        name=f"image_{count}_{len(tables)}",
    )(*inputs)


def add_kernel(one_ref, *refs):
    total = one_ref[...].astype(jnp.float32)
    for ref in refs[:-1]:
        total += ref[...].astype(jnp.float32)
    refs[-1][...] = total.astype(refs[-1].dtype)


def add_rounded(*parts):
    return pl.pallas_call(
        add_kernel,
        in_specs=[pl.BlockSpec(memory_space=VMEM)] * len(parts),
        out_specs=pl.BlockSpec(memory_space=VMEM),
        out_shape=jax.ShapeDtypeStruct(parts[0].shape, jnp.bfloat16),
        compiler_params=pltpu.CompilerParams(vmem_limit_bytes=24 << 20),
        name="add",
    )(*parts)


def add_up(*parts):
    return sum(part.astype(jnp.float32) for part in parts)


def final_kernel(scale, mine_ref, other_ref, out_ref):
    blk = lax.axis_index("blk")
    count = mine_ref.shape[1]
    source = lax.broadcasted_iota(jnp.int32, (2 * count, 2 * count), 0)
    target = lax.broadcasted_iota(jnp.int32, (2 * count, 2 * count), 1)
    wanted = jnp.where(source < count, 2 * source + blk, 2 * (source - count) + 1 - blk)
    place = (wanted == target).astype(jnp.bfloat16)
    rest = jnp.concatenate([mine_ref[...], other_ref[...].astype(jnp.float32)], axis=1) * scale
    total = jnp.zeros(out_ref.shape, jnp.float32)
    for _ in range(2):
        term = rest.astype(jnp.bfloat16)
        total += jnp.dot(term, place, preferred_element_type=jnp.float32)
        rest = rest - term.astype(jnp.float32)
    out_ref[...] = total


def interleave(mine, other, scale):
    return pl.pallas_call(
        functools.partial(final_kernel, scale),
        in_specs=[pl.BlockSpec(memory_space=VMEM)] * 2,
        out_specs=pl.BlockSpec(memory_space=VMEM),
        out_shape=jax.ShapeDtypeStruct((mine.shape[0], 2 * mine.shape[1]), jnp.float32),
        compiler_params=pltpu.CompilerParams(vmem_limit_bytes=24 << 20),
        name="interleave",
    )(mine, other)


def shift(value, axis, by):
    count = lax.axis_size(axis)
    return lax.ppermute(value, axis, [(one, (one + by) % count) for one in range(count)])


def swap(value, axis, bits, members=None):
    members = range(lax.axis_size(axis)) if members is None else members
    return lax.ppermute(value, axis, [(one, one ^ bits) for one in members])


def shards(
    visibilities, row_kernel, col_kernel, block_mask, tile_counts, tile_ids, tile_planes, w_values
):
    slots = tile_counts.shape[3]
    planes = w_values.shape[0]
    rows, vis_len = row_kernel.shape[4], row_kernel.shape[5]
    width = col_kernel.shape[5]
    img_count = lax.axis_size("img")
    wa_count = lax.axis_size("wa")
    full = rows * img_count
    table_r = jnp.asarray(row_table(NV // width, width), jnp.bfloat16)
    table_c = jnp.asarray(column_table(img_count, rows), jnp.bfloat16)
    own, send = gridding(
        tile_counts.reshape(slots),
        tile_ids.reshape(slots),
        tile_planes.reshape(slots),
        visibilities.reshape(2, slots, vis_len),
        block_mask.reshape(slots, -1, vis_len),
        row_kernel.reshape(slots, rows, vis_len),
        col_kernel.reshape(slots, vis_len, width),
        planes,
    )
    recv = shift(send, "blk", 1)
    groups = NV // 2 // LANES
    rotate = groups == img_count
    offsets = [3, 2, 0] if rotate else list(range(groups))
    neighbours = [0, 1] if rotate else [0]
    screen, middle, table_r, *columns = screens(
        offsets, neighbours, rotate, w_values, table_r, table_c
    )

    def over_wa(part):
        return [shift(part[by], "wa", by) for by in range(1, wa_count)]

    if rotate:
        outer, far, beside, here = first_images(
            [3, 2, 1, 0], 2, wa_count, own, recv, table_r, columns[0], screen, middle
        )
        from_beside = swap(beside, "img", 1)
        outer = add_rounded(outer[0], *over_wa(outer))
        far = add_rounded(far[0], *over_wa(far))
        from_outer = swap(outer, "img", 3)
        from_far = swap(far, "img", 2)
        (here,) = images(1, wa_count, 2, [here, from_beside], columns, screen, middle)
        total = add_up(here[0], *over_wa(here), from_outer, from_far)
    else:
        rowdft = row_transform(offsets, rotate, own, recv, table_r)
        parts = images(groups, wa_count, 0, rowdft, columns, screen, middle)
        part = jnp.stack(parts, axis=1)
        held = add_rounded(part[0], *over_wa(part))
        held = jnp.swapaxes(held, 0, 1).reshape(full // wa_count, img_count, -1)
        held = jnp.roll(jnp.swapaxes(held, 0, 1), -lax.axis_index("img"), axis=0)
        total = add_up(held[0], *(shift(held[by], "img", by) for by in range(1, img_count)))
    blk = lax.axis_index("blk")
    total = total.reshape(2, total.shape[0] // 2, total.shape[1])
    mine = lax.dynamic_index_in_dim(total, blk, 0, keepdims=False)
    other = lax.dynamic_index_in_dim(total, 1 - blk, 0, keepdims=False)
    other = shift(other.astype(jnp.bfloat16), "blk", 1)
    return interleave(mine, other, 1.0 / math.sqrt(full * NV * planes * wa_count))


def solution(mesh):
    in_specs = (
        P(None, ("parts", "img"), "wa", "blk", None, None),
        P(("parts", "img"), "wa", "blk", None, None, None),
        P(("parts", "img"), "wa", "blk", None, None, None),
        P(("parts", "img"), "wa", "blk", None, None, None),
        P(("parts", "img"), "wa", "blk", None),
        P(("parts", "img"), "wa", "blk", None),
        P(("parts", "img"), "wa", "blk", None),
        P(("parts", "wa")),
    )
    out_specs = P(("parts", "wa", "blk"), "img")
    return jax.shard_map(shards, mesh=mesh, in_specs=in_specs, out_specs=out_specs, check_vma=False)
```
